32 devices in a mesh: dp: 4 (over x, core), context: 8 (over z, y).
Axes of the slice: x: 2, y: 2, z: 4, core: 2. Of those that a mesh axis runs over, the one named last changes fastest.
Arguments:
- queries: bfloat16 [4, 2560, 4096], P('dp', 'context'), may hold values from -6 to 6
- keys: bfloat16 [4, 2560, 4096], P('dp', 'context'), may hold values from -6 to 6
- values: bfloat16 [4, 2560, 4096], P('dp', 'context'), may hold values from -6 to 6
- gain: float32 [4096], replicated, may hold values from 0.1 to 1.9
- out_grad: bfloat16 [4, 2560, 4096], P('dp', 'context'), may hold values from -6 to 6
Outputs:
- output: bfloat16 [4, 2560, 4096], P('dp', 'context')
- query_grad: bfloat16 [4, 2560, 4096], P('dp', 'context')
- key_grad: bfloat16 [4, 2560, 4096], P('dp', 'context')
- value_grad: bfloat16 [4, 2560, 4096], P('dp', 'context')
- gain_grad: float32 [4096], replicated
The draws below stay inside these ranges and needn't reach their ends.
All inputs are finite; a program needn't handle non-finite values.
Results may differ from the reference program's by a relative error of at most 0.0064.
Values may be sent and summed in bfloat16 or wider, within the bound.
No kernel may reach another device: no remote copies, remote signals or barrier semaphores. Data moves between devices by JAX's collectives and lax.ppermute only.
A program may use at most 192 MiB of HBM per device.

```python
import jax
import jax.numpy as jnp
from jax import lax

HEADS = 32
HD = 128
TOK_DEV = 320
FEAT = 4096
SEQS = 4
LENGTH = 2560
N_CONTEXT = 8


def block_levels(key, extent, shards, smallest, largest):
    factor_of = 1.0
    for axis_at, parts in shards:
        draws = jax.random.uniform(jax.random.fold_in(jax.random.fold_in(key, 6), axis_at), (parts,), jnp.float32, smallest / len(shards), largest / len(shards))
        factor_of = factor_of * jnp.repeat(jnp.exp(draws), extent[axis_at] // parts).reshape((-1,) + (1,) * (len(extent) - 1 - axis_at))
    return factor_of


def gaussian(key, shape, scale, limit, cuts=(), kind=jnp.bfloat16):
    array = scale * jax.random.normal(key, shape, jnp.float32)
    if cuts:
        array = array * block_levels(key, shape, cuts, -0.22, 0.18)
    return jnp.clip(array, -limit, limit).astype(kind)


def setup_inputs(seed: int = 0) -> dict:
    seeds = jax.random.split(jax.random.key(seed), 6)
    return {
        "queries": gaussian(seeds[0], (SEQS, LENGTH, FEAT), 1.0, 6.0, ((0, 4), (1, 8))),
        "keys": gaussian(seeds[1], (SEQS, LENGTH, FEAT), 1.0, 6.0, ((0, 4), (1, 8))),
        "values": gaussian(seeds[2], (SEQS, LENGTH, FEAT), 1.0, 6.0, ((0, 4), (1, 8))),
        "gain": jnp.clip(1.0 + 0.18 * jax.random.normal(seeds[3], (FEAT,), jnp.float32), 0.1, 1.9),
        "out_grad": gaussian(seeds[4], (SEQS, LENGTH, FEAT), 1.0, 6.0, ((0, 4), (1, 8))),
    }


epsilon = 1e-06

def preceding_sum(terms):
    totals = jnp.cumsum(terms, 0)
    return jnp.concatenate([jnp.zeros_like(terms[:1]), totals[:-1]], 0)

def one_sequence(pack, gain):
    query_all, key_all, value_all, grad_all = pack
    shape4 = (N_CONTEXT, TOK_DEV, HEADS, HD)
    local_query_rows = query_all.reshape(shape4).astype(jnp.float32)
    local_key_rows = key_all.reshape(shape4).astype(jnp.float32)
    local_value_rows = value_all.reshape(shape4).astype(jnp.float32)
    causal = lax.broadcasted_iota(jnp.int32, (TOK_DEV, TOK_DEV), 0) >= lax.broadcasted_iota(jnp.int32, (TOK_DEV, TOK_DEV), 1)
    block_state = jnp.einsum('cthk,cthv->chkv', local_key_rows, local_value_rows).astype(jnp.bfloat16)
    prior_state = preceding_sum(block_state.astype(jnp.float32))
    preceding_block = prior_state.astype(jnp.bfloat16).astype(jnp.float32)
    scores = jnp.einsum('cthk,cshk->chts', local_query_rows, local_key_rows)
    attn_weights = jnp.where(causal, scores, 0.0).astype(jnp.bfloat16).astype(jnp.float32)
    mixed_out = jnp.einsum('chts,cshv->cthv', attn_weights, local_value_rows) + jnp.einsum('cthk,chkv->cthv', local_query_rows, preceding_block)
    mixed_out = mixed_out.reshape(N_CONTEXT * TOK_DEV, HEADS * HD)
    inv_rms = lax.rsqrt(lax.optimization_barrier(jnp.mean(mixed_out * mixed_out, -1, keepdims=True)) + epsilon)
    normed = mixed_out * inv_rms
    output = (normed * gain).astype(jnp.bfloat16)
    grad_out = grad_all.astype(jnp.float32)
    gain_part = lax.optimization_barrier(jnp.sum(grad_out * normed, 0))
    scaled = gain * grad_out
    centered_input = lax.optimization_barrier(jnp.mean(scaled * mixed_out, -1, keepdims=True))
    mixed_gradient = (inv_rms * scaled - mixed_out * inv_rms * inv_rms * inv_rms * centered_input).astype(jnp.bfloat16)
    mixed_gradient = mixed_gradient.reshape(shape4).astype(jnp.float32)
    d_weights = jnp.where(causal, jnp.einsum('cthv,cshv->chts', mixed_gradient, local_value_rows), 0.0).astype(jnp.bfloat16).astype(jnp.float32)
    state_grad = jnp.einsum('cthk,cthv->chkv', local_query_rows, mixed_gradient).astype(jnp.bfloat16).astype(jnp.float32)
    later_state = preceding_sum(state_grad[::-1])[::-1]
    following_block = later_state.astype(jnp.bfloat16).astype(jnp.float32)
    query_grad = jnp.einsum('chts,cshk->cthk', d_weights, local_key_rows) + jnp.einsum('cthv,chkv->cthk', mixed_gradient, preceding_block)
    key_grad = jnp.einsum('chts,cthk->cshk', d_weights, local_query_rows) + jnp.einsum('cthv,chkv->cthk', local_value_rows, following_block)
    value_grad = jnp.einsum('chts,cthv->cshv', attn_weights, mixed_gradient) + jnp.einsum('cthk,chkv->cthv', local_key_rows, following_block)
    flat = (N_CONTEXT * TOK_DEV, HEADS * HD)
    return (output, query_grad.reshape(flat).astype(jnp.bfloat16), key_grad.reshape(flat).astype(jnp.bfloat16), value_grad.reshape(flat).astype(jnp.bfloat16), gain_part)

def reference(queries, keys, values, gain, out_grad):
    results = lax.map(lambda pack: one_sequence(pack, gain), (queries, keys, values, out_grad))
    output, query_grad, key_grad, value_grad, gain_parts = results
    return (output, query_grad, key_grad, value_grad, lax.optimization_barrier(jnp.sum(gain_parts, 0)))
```

```python
import functools

import jax
import jax.numpy as jnp
from jax import lax
from jax.experimental import pallas as pl
from jax.experimental.pallas import tpu as pltpu
from jax.sharding import PartitionSpec as P

HD = 128
EPSILON = 1e-06
BF16 = jnp.bfloat16
F32 = jnp.float32
VMEM_LIMIT = 40 * 1024 * 1024


def dot(a, b, contract):
    return lax.dot_general(a, b, ((contract[:1], contract[1:]), ((), ())), preferred_element_type=F32)


def divisor(n, choices):
    return next(c for c in choices if n % c == 0)


def lanes(head):
    return slice(head * HD, (head + 1) * HD)


class Layout:
    def __init__(self, tokens, features, members):
        self.tokens = tokens
        self.heads = features // HD
        self.members = members
        self.per_piece = self.heads // members
        self.per_step = divisor(self.per_piece, (4, 2, 1))
        self.steps = self.per_piece // self.per_step
        self.grid = (members, self.steps)

    def natural(self):
        steps = self.steps
        return pl.BlockSpec((self.tokens, self.per_step * HD), lambda k, j, r: (0, (r[0] ^ k) * steps + j))

    def row(self):
        steps = self.steps
        return pl.BlockSpec((1, self.per_step * HD), lambda k, j, r: (0, (r[0] ^ k) * steps + j))

    def piece(self, mine):
        last = self.steps - 1
        return pl.BlockSpec(
            (self.per_step, HD, HD),
            lambda k, j, r: (jnp.where(k == mine, j, jnp.where(k > mine, last, 0)), 0, 0),
        )

    def pieces(self):
        return [self.piece(k) for k in range(self.members)]

    def whole(self):
        return pl.BlockSpec((self.tokens, HD), lambda k, j, r: (0, 0))

    def wide(self, kind):
        return jax.ShapeDtypeStruct((self.tokens, self.heads * HD), kind)

    def narrow(self):
        return jax.ShapeDtypeStruct((self.tokens, HD), F32)

    def piece_shapes(self):
        return [jax.ShapeDtypeStruct((self.per_piece, HD, HD), BF16)] * self.members

    def call(self, body, rank, operands, in_specs, out_specs, out_shape, macs, moved, scratch=()):
        return pl.pallas_call(
            body,
            grid_spec=pltpu.PrefetchScalarGridSpec(
                num_scalar_prefetch=1,
                grid=self.grid,
                in_specs=in_specs,
                out_specs=out_specs,
                scratch_shapes=list(scratch),
            ),
            out_shape=out_shape,
            compiler_params=pltpu.CompilerParams(vmem_limit_bytes=VMEM_LIMIT),
            cost_estimate=pl.CostEstimate(flops=2 * macs, bytes_accessed=moved, transcendentals=0),
        )(rank, *operands)


def for_piece(layout, refs, act):
    for k in range(layout.members):

        @pl.when(pl.program_id(0) == k)
        def _(k=k):
            act(refs[k])


def block_states(layout, rank, keys, values):
    def body(r, k_ref, v_ref, *outs):
        def act(out):
            for h in range(layout.per_step):
                out[h] = dot(k_ref[:, lanes(h)], v_ref[:, lanes(h)], (0, 0)).astype(BF16)

        for_piece(layout, outs, act)

    size = layout.tokens * layout.heads * HD
    return layout.call(
        body, rank, (keys, values), [layout.natural()] * 2, layout.pieces(), layout.piece_shapes(),
        size * HD, 4 * size,
    )


def causal_mask(tokens, upper):
    rows = lax.broadcasted_iota(jnp.int32, (tokens, tokens), 0)
    columns = lax.broadcasted_iota(jnp.int32, (tokens, tokens), 1)
    return rows <= columns if upper else rows >= columns


def within_block(layout, rank, queries, keys, values):
    def body(r, q_ref, k_ref, v_ref, o_ref):
        keep = causal_mask(layout.tokens, False)
        for h in range(layout.per_step):
            scores = dot(q_ref[:, lanes(h)], k_ref[:, lanes(h)], (1, 1))
            weights = jnp.where(keep, scores, 0.0).astype(BF16)
            o_ref[:, lanes(h)] = dot(weights, v_ref[:, lanes(h)], (1, 0))

    size = layout.tokens * layout.heads * HD
    return layout.call(
        body, rank, (queries, keys, values), [layout.natural()] * 3, layout.natural(), layout.wide(F32),
        2 * size * layout.tokens, 10 * size,
    )


def mix(layout, rank, inner, queries, out_grad, gain, prior):
    def body(r, o_ref, q_ref, g_ref, gain_ref, *refs):
        states, (m_ref, square_ref, cross_ref) = refs[: layout.members], refs[layout.members :]

        @pl.when((pl.program_id(0) == 0) & (pl.program_id(1) == 0))
        def _():
            square_ref[...] = jnp.zeros_like(square_ref)
            cross_ref[...] = jnp.zeros_like(cross_ref)

        def act(state):
            square, cross = square_ref[...], cross_ref[...]
            for h in range(layout.per_step):
                mixed = o_ref[:, lanes(h)] + dot(q_ref[:, lanes(h)], state[h], (1, 0))
                m_ref[:, lanes(h)] = mixed
                square = square + mixed * mixed
                cross = cross + gain_ref[:, lanes(h)] * g_ref[:, lanes(h)].astype(F32) * mixed
            square_ref[...] = square
            cross_ref[...] = cross

        for_piece(layout, states, act)

    size = layout.tokens * layout.heads * HD
    return layout.call(
        body, rank, (inner, queries, out_grad, gain, *prior),
        [layout.natural()] * 3 + [layout.row()] + layout.pieces(),
        [layout.natural(), layout.whole(), layout.whole()],
        [layout.wide(F32), layout.narrow(), layout.narrow()],
        size * HD, 12 * size,
    )


def mixed_gradients(layout, rank, mixed, queries, out_grad, gain, square, cross):
    features = layout.heads * HD

    def body(r, m_ref, q_ref, g_ref, gain_ref, square_ref, cross_ref, d_ref, inv_ref, *rest):
        outs, factor_ref = rest[:-1], rest[-1]

        @pl.when((pl.program_id(0) == 0) & (pl.program_id(1) == 0))
        def _():
            mean = jnp.sum(square_ref[...], -1, keepdims=True) / features
            inv = lax.rsqrt(mean + EPSILON)
            centered = jnp.sum(cross_ref[...], -1, keepdims=True) / features
            inv_ref[...] = jnp.broadcast_to(inv, inv_ref.shape)
            factor_ref[...] = jnp.broadcast_to(inv * inv * inv * centered, factor_ref.shape)

        def act(out):
            for h in range(layout.per_step):
                scaled = gain_ref[:, lanes(h)] * g_ref[:, lanes(h)].astype(F32)
                grad = (inv_ref[...] * scaled - m_ref[:, lanes(h)] * factor_ref[...]).astype(BF16)
                d_ref[:, lanes(h)] = grad
                out[h] = dot(q_ref[:, lanes(h)], grad, (0, 0)).astype(BF16)

        for_piece(layout, outs, act)

    size = layout.tokens * layout.heads * HD
    return layout.call(
        body, rank, (mixed, queries, out_grad, gain, square, cross),
        [layout.natural()] * 3 + [layout.row(), layout.whole(), layout.whole()],
        [layout.natural(), layout.whole()] + layout.pieces(),
        [layout.wide(BF16), layout.narrow()] + layout.piece_shapes(),
        size * HD, 10 * size, [pltpu.VMEM((layout.tokens, HD), F32)],
    )


def normed_output(layout, rank, mixed, out_grad, gain, inv):
    def body(r, m_ref, g_ref, gain_ref, inv_ref, o_ref, part_ref):
        for h in range(layout.per_step):
            normed = m_ref[:, lanes(h)] * inv_ref[...]
            o_ref[:, lanes(h)] = (normed * gain_ref[:, lanes(h)]).astype(BF16)
            part_ref[:, lanes(h)] = jnp.sum(g_ref[:, lanes(h)].astype(F32) * normed, 0, keepdims=True)

    size = layout.tokens * layout.heads * HD
    return layout.call(
        body, rank, (mixed, out_grad, gain, inv),
        [layout.natural()] * 2 + [layout.row(), layout.whole()],
        [layout.natural(), layout.row()],
        [layout.wide(BF16), jax.ShapeDtypeStruct((1, layout.heads * HD), F32)],
        0, 8 * size,
    )


def inner_gradients(layout, rank, queries, keys, values, d_mixed, prior):
    def body(r, q_ref, k_ref, v_ref, d_ref, *refs):
        states, (dq_ref, dk_ref, dv_ref) = refs[: layout.members], refs[layout.members :]
        lower = causal_mask(layout.tokens, False)
        upper = causal_mask(layout.tokens, True)

        def act(state):
            for h in range(layout.per_step):
                q, k, v, d = (ref[:, lanes(h)] for ref in (q_ref, k_ref, v_ref, d_ref))
                d_weights = jnp.where(lower, dot(d, v, (1, 1)), 0.0).astype(BF16)
                dq_ref[:, lanes(h)] = (dot(d_weights, k, (1, 0)) + dot(d, state[h], (1, 1))).astype(BF16)
                d_turned = jnp.where(upper, dot(v, d, (1, 1)), 0.0).astype(BF16)
                dk_ref[:, lanes(h)] = dot(d_turned, q, (1, 0))
                turned = jnp.where(upper, dot(k, q, (1, 1)), 0.0).astype(BF16)
                dv_ref[:, lanes(h)] = dot(turned, d, (1, 0))

        for_piece(layout, states, act)

    size = layout.tokens * layout.heads * HD
    return layout.call(
        body, rank, (queries, keys, values, d_mixed, *prior),
        [layout.natural()] * 4 + layout.pieces(),
        [layout.natural()] * 3,
        [layout.wide(BF16), layout.wide(F32), layout.wide(F32)],
        size * (6 * layout.tokens + HD), 18 * size,
    )


def outer_gradients(layout, rank, keys, values, dk_inner, dv_inner, later):
    def body(r, k_ref, v_ref, dki_ref, dvi_ref, *refs):
        states, (dk_ref, dv_ref) = refs[: layout.members], refs[layout.members :]

        def act(state):
            for h in range(layout.per_step):
                k, v = k_ref[:, lanes(h)], v_ref[:, lanes(h)]
                dk_ref[:, lanes(h)] = (dki_ref[:, lanes(h)] + dot(v, state[h], (1, 1))).astype(BF16)
                dv_ref[:, lanes(h)] = (dvi_ref[:, lanes(h)] + dot(k, state[h], (1, 0))).astype(BF16)

        for_piece(layout, states, act)

    size = layout.tokens * layout.heads * HD
    return layout.call(
        body, rank, (keys, values, dk_inner, dv_inner, *later),
        [layout.natural()] * 4 + layout.pieces(),
        [layout.natural()] * 2,
        [layout.wide(BF16)] * 2,
        2 * size * HD, 16 * size,
    )


def swap(array, axis, size, k):
    return lax.ppermute(array, axis, [(c, c ^ k) for c in range(size)])


def carried(pieces, rank, size, members, forward):
    order = [k for k in range(members - 1, 0, -1)]
    got = {k: swap(pieces[k], "context", size, k) for k in order}
    got = {k: array.astype(F32) for k, array in [(0, pieces[0]), *got.items()]}
    total = sum(got[k] for k in range(members)).astype(BF16)
    base = jnp.zeros(total.shape, F32)
    for far in range(1, size // members):
        hop = far * members
        if forward:
            pairs = [(c, c + hop) for c in range(size - hop)]
        else:
            pairs = [(c + hop, c) for c in range(size - hop)]
        base = base + lax.ppermute(total, "context", pairs).astype(F32)
    result = [None] * members
    for k in [*order, 0]:
        held = base
        for j in range(members):
            if j != k:
                ahead = (rank ^ j) < (rank ^ k) if forward else (rank ^ j) > (rank ^ k)
                held = held + jnp.where(ahead, got[j], 0.0)
        held = held.astype(BF16)
        result[k] = swap(held, "context", size, k) if k else held
    return result


def summed(part, axis, size):
    if size & (size - 1):
        return lax.psum(part, axis)
    stride = 1
    while stride < size:
        span = divisor(size // stride, (4, 2))
        part = sum((swap(part, axis, size, k * stride) for k in range(1, span)), part)
        stride *= span
    return part


def shards(dp, context, queries, keys, values, gain, out_grad):
    tokens, features = queries.shape[1:]
    members = divisor(context, (4, 2, 1))
    layout = Layout(tokens, features, members)
    rank = lax.axis_index("context") % members
    place = rank.astype(jnp.int32).reshape(1)
    q, k, v, g = (array[0] for array in (queries, keys, values, out_grad))
    gain_row = gain.reshape(1, features)

    states = block_states(layout, place, k, v)
    inner = within_block(layout, place, q, k, v)
    prior = carried(states, rank, context, members, True)
    mixed, square, cross = mix(layout, place, inner, q, g, gain_row, prior)
    d_mixed, inv, *state_grads = mixed_gradients(layout, place, mixed, q, g, gain_row, square, cross)
    later = carried(state_grads, rank, context, members, False)
    output, gain_part = normed_output(layout, place, mixed, g, gain_row, inv)
    gain_part = gain_part.reshape(features // HD, HD)
    gain_grad = summed(summed(gain_part, "dp", dp), "context", context)
    query_grad, dk_inner, dv_inner = inner_gradients(layout, place, q, k, v, d_mixed, prior)
    key_grad, value_grad = outer_gradients(layout, place, k, v, dk_inner, dv_inner, later)
    return output[None], query_grad[None], key_grad[None], value_grad[None], gain_grad.reshape(features)


def solution(mesh):
    sharded = P("dp", "context", None)
    return jax.shard_map(
        functools.partial(shards, mesh.shape["dp"], mesh.shape["context"]),
        mesh=mesh,
        in_specs=(sharded, sharded, sharded, P(), sharded),
        out_specs=(sharded, sharded, sharded, sharded, P()),
        check_vma=False,
    )
```

```python
import functools

import jax
import jax.numpy as jnp
from jax import lax
from jax.experimental import pallas as pl
from jax.experimental.pallas import tpu as pltpu
from jax.sharding import PartitionSpec as P

HD = 128
EPSILON = 1e-06
BF16 = jnp.bfloat16
F32 = jnp.float32
CHUNKS = 2
HINTS = {"mix": 10, "outer_gradients": 10}
VMEM_LIMIT = 14 * 1024 * 1024


def dot(a, b, contract):
    return lax.dot_general(a, b, ((contract[:1], contract[1:]), ((), ())), preferred_element_type=F32)


def divisor(n, choices):
    return next(c for c in choices if n % c == 0)


def lanes(head):
    return slice(head * HD, (head + 1) * HD)


def resident(array):
    return pltpu.with_memory_space_constraint(array, pltpu.VMEM)


def pairs_of(count):
    step = 2 if count % 2 == 0 else 1
    return [range(h, h + step) for h in range(0, count, step)]


def rows_of(head, offset=0):
    return slice(offset + head * HD, offset + (head + 1) * HD)


def span(heads):
    return slice(heads[0] * HD, (heads[-1] + 1) * HD)


def diagonal(blocks):
    if len(blocks) == 1:
        return blocks[0]
    zero = jnp.zeros_like(blocks[0])
    return jnp.concatenate([jnp.concatenate([blocks[0], zero], 1), jnp.concatenate([zero, blocks[1]], 1)], 0)


HBM_WHOLE = pl.BlockSpec(memory_space=pl.ANY)


class Layout:
    def __init__(self, tokens, features, members, chunks):
        self.tokens = tokens
        self.features = features
        self.heads = features // HD
        self.members = members
        self.chunks = chunks
        self.count = self.heads // members // chunks
        self.width = self.count * HD
        self.size = self.count * members * tokens * HD

    def wide(self, chunk, first=0):
        chunks = self.chunks
        return pl.BlockSpec((self.tokens, self.width), lambda k, r: (0, (r[0] ^ (k + first)) * chunks + chunk))

    def columns(self, r, piece, chunk):
        return pl.ds(pl.multiple_of(((r[0] ^ piece) * self.chunks + chunk) * self.width, self.width), self.width)

    def wide_shape(self, kind=BF16):
        return jax.ShapeDtypeStruct((self.tokens, self.features), kind)

    def row_shape(self):
        return jax.ShapeDtypeStruct((1, self.features), F32)

    def kept(self, kind):
        return pltpu.VMEM((self.members, self.tokens, self.width), kind)

    def kept_row(self):
        return pltpu.VMEM((self.members, 1, self.width), F32)

    def narrow(self):
        return pltpu.VMEM((self.tokens, HD), F32)

    def piece(self, extra=0):
        return pltpu.VMEM((self.count * HD + extra, HD), BF16)

    def cut(self):
        return self.tokens // 256 * 256 if self.tokens > 256 and self.tokens % 256 % 16 == 0 else self.tokens

    def weights(self):
        cut, rest = self.cut(), max(self.tokens - self.cut(), 16)
        lead = (self.members, self.count)
        return [pltpu.VMEM((*lead, self.tokens, cut), BF16), pltpu.VMEM((*lead, rest, rest), BF16)]

    def token(self):
        return pltpu.VMEM((8, HD), F32)

    def call(self, name, body, rank, streamed, held, outs, after=(), into=(), macs=0, moved=0, scratch=(), grid=(1,)):
        whole = pl.BlockSpec(memory_space=pltpu.VMEM)
        unread = pl.BlockSpec(memory_space=pl.ANY)
        operands = [pltpu.with_memory_space_constraint(a, pltpu.HBM) for a in streamed]
        operands += [resident(a) for a in [*held, *after]]
        operands += [pltpu.with_memory_space_constraint(a, memory) for a, _, memory in into]
        first = 1 + len(streamed) + len(held) + len(after)
        used = len(streamed) + len(held)
        skipped = len(after) + len(into)

        def kernel(r, *refs):
            body(r, *refs[:used], *refs[used + skipped :])

        return pl.pallas_call(
            kernel,
            name=name,
            grid_spec=pltpu.PrefetchScalarGridSpec(
                num_scalar_prefetch=1,
                grid=grid,
                in_specs=[unread] * len(streamed) + [whole] * len(held) + [unread] * skipped,
                out_specs=[whole if s is None else s for _, s in outs],
                scratch_shapes=list(scratch),
            ),
            out_shape=[s for s, _ in outs],
            input_output_aliases={first + n: at for n, (_, at, _) in enumerate(into)},
            compiler_params=pltpu.CompilerParams(vmem_limit_bytes=VMEM_LIMIT),
            cost_estimate=pl.CostEstimate(
                flops=int(HINTS.get(name, 0) * 1e9) + 1, bytes_accessed=int(HINTS.get(name, 0) * 3.6e6) + 1, transcendentals=0
            ),
        )(rank, *operands)


def for_piece(refs, act):
    for k, ref in enumerate(refs):

        @pl.when(pl.program_id(0) == k)
        def _(ref=ref):
            act(ref)


def block_states(layout, rank, keys, values, chunk):
    members = layout.members

    def body(r, k_hbm, v_hbm, k_out, v_out, *refs):
        outs, sems = refs[:members], refs[members]
        copies = []
        for piece in range(members):
            at = layout.columns(r, piece, chunk)
            copies.append(pltpu.make_async_copy(k_hbm.at[:, at], k_out.at[piece], sems.at[0, piece]))
            copies.append(pltpu.make_async_copy(v_hbm.at[:, at], v_out.at[piece], sems.at[1, piece]))
        for copy in copies:
            copy.start()
        for piece in range(members):
            copies[2 * piece].wait()
            copies[2 * piece + 1].wait()
            states = [dot(k_out[piece, :, lanes(h)], v_out[piece, :, lanes(h)], (0, 0)) for h in range(layout.count)]
            for h, state in enumerate(states):
                outs[piece][lanes(h), :] = state.astype(BF16)

    k, v, *states = layout.call(
        "block_states", body, rank, [keys, values], [],
        [(layout.kept(BF16), None)] * 2 + [(layout.piece(), None)] * members,
        macs=layout.size * HD, moved=4 * layout.size, scratch=[pltpu.SemaphoreType.DMA((2, members))],
    )
    return k, v, states


def masked(product):
    rows = lax.broadcasted_iota(jnp.int32, product.shape, 0)
    columns = lax.broadcasted_iota(jnp.int32, product.shape, 1)
    return jnp.where(rows >= columns, product, 0.0).astype(BF16)


def masked_product(a, b, cut):
    blocks = [masked(dot(a, b[:cut], (1, 1)))]
    if cut < a.shape[0]:
        blocks.append(masked(dot(a[cut:], b[cut:], (1, 1))))
    return blocks


def store_product(out, at, blocks, b, cut, add=None):
    rows, columns = at[1:] if len(at) == 3 else at
    lead = at[:-2]
    full = dot(blocks[0], b[:cut], (1, 0))
    full = full if add is None else full + add
    out[(*lead, slice(0, cut), columns)] = full[:cut].astype(out.dtype)
    if len(blocks) > 1:
        out[(*lead, slice(cut, None), columns)] = (full[cut:] + dot(blocks[1], b[cut:], (1, 0))).astype(out.dtype)


def store_turned(out, at, blocks, b, cut):
    lead, columns = at[:-2], at[-1]
    out[(*lead, slice(0, cut), columns)] = dot(blocks[0], b, (0, 0))
    if len(blocks) > 1:
        out[(*lead, slice(cut, None), columns)] = dot(blocks[1], b[cut:], (0, 0))


def within_block(layout, rank, queries, out_grad, gain, keys, values, chunk, after):
    members = layout.members

    def body(r, q_hbm, g_hbm, gain_ref, k_ref, v_ref, q_out, g_out, gain_out, o_ref, *refs):
        w_refs, sems = refs[:-1], refs[-1]
        q_copies, g_copies = [], []
        for piece in range(members):
            at = layout.columns(r, piece, chunk)
            q_copies.append(pltpu.make_async_copy(q_hbm.at[:, at], q_out.at[piece], sems.at[0, piece]))
            g_copies.append(pltpu.make_async_copy(g_hbm.at[:, at], g_out.at[piece], sems.at[1, piece]))
        for copy in q_copies + g_copies:
            copy.start()
        for piece in range(members):
            gain_out[piece] = gain_ref[:, layout.columns(r, piece, chunk)]
            q_copies[piece].wait()
            weights = []
            for h in range(layout.count):
                weights.append(masked_product(q_out[piece, :, lanes(h)], k_ref[piece, :, lanes(h)], layout.cut()))
            for h in range(layout.count):
                for w_ref, block in zip(w_refs, weights[h]):
                    w_ref[piece, h] = block
                store_product(o_ref, (piece, slice(None), lanes(h)), weights[h], v_ref[piece, :, lanes(h)], layout.cut())
        for copy in g_copies:
            copy.wait()

    return layout.call(
        "within_block", body, rank, [queries, out_grad], [gain, keys, values],
        [(layout.kept(BF16), None)] * 2 + [(layout.kept_row(), None), (layout.kept(F32), None)]
        + [(shape, None) for shape in layout.weights()],
        after=after, macs=2 * layout.size * layout.tokens, moved=4 * layout.size, scratch=[pltpu.SemaphoreType.DMA((2, members))],
    )


def mix(layout, rank, kept, prior, jobs, mixed, sums):
    chunks = sorted({c for c, _ in jobs})
    fields = [kept[c][n] for c in chunks for n in (3, 0, 1, 2)]
    states = [prior[c][k][0] for c, k in jobs]
    old = [(n, mixed[c]) for n, c in enumerate(chunks) if c in mixed]

    def body(r, *refs):
        fields_in, refs = refs[: len(fields)], refs[len(fields) :]
        state_refs, refs = refs[: len(jobs)], refs[len(jobs) :]
        before, (*m_refs, square_ref, cross_ref) = refs[: len(sums)], refs[len(sums) :]
        square = before[0][...] if sums else jnp.zeros(square_ref.shape, F32)
        cross = before[1][...] if sums else jnp.zeros(cross_ref.shape, F32)
        for (c, piece), state in zip(jobs, state_refs, strict=True):
            n, offset = chunks.index(c), prior[c][piece][1]
            o_ref, q_ref, g_ref, gain_ref = fields_in[4 * n : 4 * n + 4]
            products = []
            for heads in pairs_of(layout.count):
                block = diagonal([state[rows_of(h, offset), :] for h in heads])
                both = dot(q_ref[piece, :, span(heads)], block, (1, 0))
                products += [both[:, lanes(m)] for m in range(len(heads))]
            for h in range(layout.count):
                at = (piece, slice(None), lanes(h))
                value = o_ref[at] + products[h]
                m_refs[n][at] = value
                square = square + value * value
                cross = cross + gain_ref[piece, :, lanes(h)] * g_ref[at].astype(F32) * value
        square_ref[...] = square
        cross_ref[...] = cross

    *outs, square, cross = layout.call(
        "mix", body, rank, [], [*fields, *states, *sums],
        [(layout.kept(F32), None)] * len(chunks) + [(layout.narrow(), None)] * 2,
        into=[(a, n, pltpu.VMEM) for n, a in old], macs=layout.size * HD, moved=layout.size,
    )
    return {**mixed, **dict(zip(chunks, outs, strict=True))}, [square, cross]


def norm_factors(layout, rank, square, cross):
    def body(r, square_ref, cross_ref, inv_ref, factor_ref):
        mean = jnp.sum(square_ref[...], -1, keepdims=True) / layout.features
        inv = lax.rsqrt(mean + EPSILON)
        centered = jnp.sum(cross_ref[...], -1, keepdims=True) / layout.features
        inv_ref[...] = jnp.broadcast_to(inv, inv_ref.shape)
        factor_ref[...] = jnp.broadcast_to(inv * inv * inv * centered, factor_ref.shape)

    return layout.call(
        "norm_factors", body, rank, [], [square, cross], [(layout.narrow(), None)] * 2, moved=layout.tokens * HD * 4
    )


def mixed_gradients(layout, rank, mixed, queries, out_grad, gain, inv, factor):
    def body(r, m_ref, q_ref, g_ref, gain_ref, inv_ref, factor_ref, d_ref, *outs):
        piece = pl.program_id(0)

        def act(out):
            for h in range(layout.count):
                at = (piece, slice(None), lanes(h))
                scaled = gain_ref[piece, :, lanes(h)] * g_ref[at].astype(F32)
                grad = (inv_ref[...] * scaled - m_ref[at] * factor_ref[...]).astype(BF16)
                d_ref[at] = grad
                out[lanes(h), :] = dot(q_ref[at], grad, (0, 0)).astype(BF16)

        for_piece(outs, act)

    d_mixed, *states = layout.call(
        "mixed_gradients", body, rank, [], [mixed, queries, out_grad, gain, inv, factor],
        [(layout.kept(BF16), None)] + [(layout.piece(), None)] * layout.members,
        macs=layout.size * HD, moved=layout.size, grid=(layout.members,),
    )
    return d_mixed, states


def normed_output(layout, rank, mixed, out_grad, gain, inv, chunk, into, after):
    members = layout.members

    def body(r, m_ref, g_ref, gain_ref, inv_ref, o_hbm, part_ref, buffer, sems):
        copies = []
        for piece in range(members):
            at = layout.columns(r, piece, chunk)
            for h in range(layout.count):
                here = (piece, slice(None), lanes(h))
                normed = m_ref[here] * inv_ref[...]
                buffer[here] = (normed * gain_ref[piece, :, lanes(h)]).astype(BF16)
                head = ((r[0] ^ piece) * layout.chunks + chunk) * layout.count + h
                part_ref[pl.ds(head, 1), :] = jnp.sum(g_ref[here].astype(F32) * normed, 0, keepdims=True)
            copies.append(pltpu.make_async_copy(buffer.at[piece], o_hbm.at[:, at], sems.at[piece]))
            copies[-1].start()
        for copy in copies:
            copy.wait()

    return layout.call(
        "normed_output", body, rank, [], [mixed, out_grad, gain, inv],
        [(layout.wide_shape(), HBM_WHOLE), (pltpu.VMEM((layout.heads, HD), F32), None)],
        into=[(a, n, m) for n, (a, m) in enumerate(zip(into, (pltpu.HBM, pltpu.VMEM)))], after=after, moved=2 * layout.size,
        scratch=[pltpu.VMEM((members, layout.tokens, layout.width), BF16), pltpu.SemaphoreType.DMA((members,))],
    )


def inner_gradients(layout, rank, weights, queries, keys, values, d_mixed, prior, chunk, part, dq, own, after):
    first, last = part

    def body(r, *refs):
        w_refs, (q_ref, k_ref, v_ref, d_ref, *refs) = refs[: len(weights)], refs[len(weights) :]
        states, (dq_ref, dk_ref, dv_ref, token_ref, state) = refs[: last - first], refs[last - first :]
        piece = pl.program_id(0) + first
        token_ref[...] = jnp.zeros_like(token_ref)

        for n, (ref, (_, offset)) in enumerate(zip(states, prior[first:last], strict=True)):

            @pl.when(pl.program_id(0) == n)
            def _(ref=ref, offset=offset):
                state[...] = ref[offset : offset + layout.count * HD, :]

        d_weights, from_prior = [], []
        for h in range(layout.count):
            at = (piece, slice(None), lanes(h))
            d_weights.append(masked_product(d_ref[at], v_ref[at], layout.cut()))
        for heads in pairs_of(layout.count):
            both = dot(d_ref[piece, :, span(heads)], diagonal([state[lanes(h), :] for h in heads]), (1, 1))
            from_prior += [both[:, lanes(n)] for n in range(len(heads))]
        for h in range(layout.count):
            at = (piece, slice(None), lanes(h))
            kept = [w_ref[piece, h] for w_ref in w_refs][: len(d_weights[h])]
            store_product(dq_ref, at[1:], d_weights[h], k_ref[at], layout.cut(), from_prior[h])
            store_turned(dk_ref, at, d_weights[h], q_ref[at], layout.cut())
            store_turned(dv_ref, at, kept, d_ref[at], layout.cut())

    return layout.call(
        "inner_gradients", body, rank, [], [*weights, queries, keys, values, d_mixed, *[a for a, _ in prior[first:last]]],
        [(layout.wide_shape(), layout.wide(chunk, first)), (layout.kept(F32), None), (layout.kept(F32), None), (layout.token(), None)],
        into=[(a, n, pltpu.HBM) for n, a in enumerate(dq)] + [(a, n + 1, pltpu.VMEM) for n, a in enumerate(own)], after=after,
        macs=layout.size * 4 * layout.tokens * (last - first) // layout.members, moved=layout.size,
        scratch=[pltpu.VMEM((layout.count * HD, HD), BF16)], grid=(last - first,),
    )


def pairwise(terms):
    while len(terms) > 1:
        terms = [a + b for a, b in zip(terms[::2], terms[1::2], strict=True)]
    return terms[0]


def outer_gradients(layout, rank, keys, values, own, later, jobs, into, extra):
    chunks = sorted({c for c, _ in jobs})
    fields = [a for c in chunks for a in (keys[c], values[c], *own[c])]
    states = [later[c][k][0] for c, k in jobs]
    count, heads_all = len(jobs), layout.heads
    gain_out = [(jax.ShapeDtypeStruct((heads_all, HD), F32), HBM_WHOLE)] if extra else []

    def body(r, *refs):
        fields_in, refs = refs[: len(fields)], refs[len(fields) :]
        state_refs, (dk_hbm, dv_hbm, *refs) = refs[:count], refs[count:]
        gain_hbm, (dk_buffer, dv_buffer, gain_buffer, sems) = refs[: len(gain_out)], refs[len(gain_out) :]
        copies = []
        if extra:
            parts = []
            for _, n in sorted((piece, n) for n, (c, piece) in enumerate(jobs) if c == chunks[-1]):
                rows = state_refs[n][-2 * heads_all :, :].astype(F32)
                parts.append(rows[:heads_all] + rows[heads_all:])
            gain_buffer[...] = pairwise(parts)
            copies.append(pltpu.make_async_copy(gain_buffer, gain_hbm[0], sems.at[2, 0]))
            copies[-1].start()
        for n, ((c, piece), state) in enumerate(zip(jobs, state_refs, strict=True)):
            at, offset = layout.columns(r, piece, c), later[c][piece][1]
            k_ref, v_ref, dki_ref, dvi_ref = fields_in[4 * chunks.index(c) : 4 * chunks.index(c) + 4]
            sums = []
            for heads in pairs_of(layout.count):
                here = (piece, slice(None), span(heads))
                block = diagonal([state[rows_of(h, offset), :] for h in heads])
                sums.append((heads, here, dot(v_ref[here], block, (1, 1)), dot(k_ref[here], block, (1, 0))))
            for heads, here, dk, dv in sums:
                dk_buffer[n, :, span(heads)] = (dki_ref[here] + dk).astype(BF16)
                dv_buffer[n, :, span(heads)] = (dvi_ref[here] + dv).astype(BF16)
            copies.append(pltpu.make_async_copy(dk_buffer.at[n], dk_hbm.at[:, at], sems.at[0, n]))
            copies.append(pltpu.make_async_copy(dv_buffer.at[n], dv_hbm.at[:, at], sems.at[1, n]))
            copies[-2].start()
            copies[-1].start()
        for copy in copies:
            copy.wait()

    return layout.call(
        "outer_gradients", body, rank, [], [*fields, *states],
        [(layout.wide_shape(), HBM_WHOLE)] * 2 + gain_out,
        into=[(a, n, pltpu.HBM) for n, a in enumerate(into)],
        macs=2 * layout.size * HD, moved=4 * layout.size,
        scratch=[pltpu.VMEM((count, layout.tokens, layout.width), BF16)] * 2
        + [pltpu.VMEM((heads_all, HD), F32), pltpu.SemaphoreType.DMA((3, count))],
    )


def swap(array, axis, size, k):
    return lax.ppermute(array, axis, [(c, c ^ k) for c in range(size)])


def gather_home(pieces, context):
    order = range(len(pieces) - 1, 0, -1)
    got = {k: swap(pieces[k], "context", context, k) for k in order}
    return [pieces[0]] + [got[k] for k in range(1, len(pieces))]


def group_total(layout, rank, got, after):
    def body(r, *refs):
        *gots, total = refs
        total[...] = sum(g[...].astype(F32) for g in gots).astype(BF16)

    return layout.call(
        "group_total", body, rank, [], got, [(layout.piece(), None)], after=after, moved=layout.count * HD * HD * 10
    )[0]


def cross_groups(total, members, context, forward):
    bases = []
    for far in range(1, context // members):
        hop = far * members
        up = [(c, c + hop) for c in range(context - hop)]
        bases.append(lax.ppermute(total, "context", up if forward else [(b, a) for a, b in up]))
    return bases


def spread(layout, rank, got, bases, forward, after, joined=(), gain=()):
    members, heads_all = layout.members, layout.heads
    extra = 2 * heads_all * len(gain)
    shift = layout.count * HD * len(joined)

    def body(r, *refs):
        gots, rest = refs[:members], refs[members:]
        lows, rest = rest[: len(bases)], rest[len(bases) :]
        joined_refs, rest = rest[: len(joined)], rest[len(joined) :]
        gains, outs = rest[: len(gain)], rest[len(gain) :]
        for n, ref in enumerate(joined_refs):
            outs[-1][n * layout.count * HD : (n + 1) * layout.count * HD, :] = ref[...]
        for h in range(layout.count):
            held = [g[rows_of(h), :].astype(F32) for g in gots]
            base = sum((low[rows_of(h), :].astype(F32) for low in lows), jnp.zeros((HD, HD), F32))
            for k in range(members):
                part = base
                for j in range(members):
                    if j != k:
                        one, other = r[0] ^ j, r[0] ^ k
                        ahead = one < other if forward else one > other
                        part = part + held[j] * ahead.astype(F32)
                outs[k][rows_of(h, shift if k == members - 1 else 0), :] = part.astype(BF16)
        for ref in gains:
            high = ref[...].astype(BF16)
            low = (ref[...] - high.astype(F32)).astype(BF16)
            for out in outs:
                rows = out.shape[0]
                out[rows - 2 * heads_all : rows - heads_all, :] = high
                out[rows - heads_all : rows, :] = low

    return layout.call(
        "spread", body, rank, [], [*got, *bases, *joined, *gain],
        [(layout.piece(extra), None)] * (members - 1) + [(layout.piece(extra + shift), None)], after=after,
        moved=layout.count * HD * HD * 18,
    )


def scatter_back(layout, rank, got, bases, context, forward, mark, between, gain=None):
    far, joined, pieces = layout.members - 1, [], []
    for c in range(layout.chunks):
        final = c == layout.chunks - 1
        mark = between(c, mark)
        rows = [gain()] if final and gain else []
        outs = spread(layout, rank, got[c], bases[c], forward, mark, joined if final else [], rows)
        mark = [outs[0]]
        joined.append(outs[far])
        order = range(far if final else far - 1, 0, -1)
        moved = {k: swap(outs[k], "context", context, k) for k in order}
        pieces.append([(moved.get(k, outs[k]), 0) for k in range(layout.members)])
    if far:
        last = pieces[-1][far][0]
        for c, chunk in enumerate(pieces):
            chunk[far] = (last, c * layout.count * HD)
    return pieces, mark


def xor_steps(axis, size, stride):
    steps = []
    while stride < size:
        steps.append((axis, size, stride))
        stride *= 2
    return steps


def added(layout, rank, one, other, after):
    def body(r, one_ref, other_ref, out_ref):
        out_ref[...] = one_ref[...] + other_ref[...]

    return layout.call(
        "gain_sum", body, rank, [], [one, other], [(pltpu.VMEM(one.shape, F32), None)], after=after, moved=one.size * 12
    )[0]


def shards(dp, context, queries, keys, values, gain, out_grad):
    tokens, features = queries.shape[1:]
    members = divisor(context, (4, 2, 1))
    layout = Layout(tokens, features, members, CHUNKS)
    chunks = range(CHUNKS)
    place = (lax.axis_index("context") % members).astype(jnp.int32).reshape(1)
    q, k, v, g = (array[0] for array in (queries, keys, values, out_grad))
    gain_row = gain.reshape(1, features)

    k_kept, v_kept, got = [], [], []
    for c in chunks:
        k_c, v_c, states = block_states(layout, place, k, v, c)
        k_kept.append(k_c)
        v_kept.append(v_c)
        got.append(gather_home(states, context))
    inner, bases, mark = [], [], []
    for c in chunks:
        total = group_total(layout, place, got[c], mark)
        bases.append(cross_groups(total, members, context, True))
        inner.append(within_block(layout, place, q, g, gain_row, k_kept[c], v_kept[c], c, [total]))
        mark = [inner[c][3]]
    prior, mark = scatter_back(layout, place, got, bases, context, True, mark, lambda c, mark: mark)
    far = members - 1
    early = [(c, k) for c in chunks[:-1] for k in range(far)]
    middle = [(CHUNKS - 1, k) for k in range(far)]
    late = [(c, far) for c in chunks]
    mixed, sums = {}, []
    for group in (early, middle, late):
        if group:
            mixed, sums = mix(layout, place, inner, prior, group, mixed, sums)
    inv, factor = norm_factors(layout, place, *sums)

    d_mixed, got = [], []
    for c in chunks:
        q_c, g_c, gain_c = inner[c][:3]
        d_c, states = mixed_gradients(layout, place, mixed[c], q_c, g_c, gain_c, inv, factor)
        d_mixed.append(d_c)
        got.append(gather_home(states, context))

    out, dq, own, gain_grad = [], [], [[] for _ in chunks], None
    regular = dp & (dp - 1) == 0 and context & (context - 1) == 0
    steps = xor_steps("dp", dp, 1) + xor_steps("context", context, members) if regular else []

    def inner_job(mark, c, part):
        nonlocal dq
        *dq, dk_c, dv_c, token = inner_gradients(
            layout, place, inner[c][4:], inner[c][0], k_kept[c], v_kept[c], d_mixed[c], prior[c], c, part, dq, own[c], mark
        )
        own[c] = [dk_c, dv_c]
        return [token]

    def gain_job(mark):
        nonlocal gain_grad
        if not steps:
            return mark
        axis, size, stride = steps.pop(0)
        gain_grad = added(layout, place, gain_grad, swap(gain_grad, axis, size, stride), mark)
        return [gain_grad]

    cuts = sorted({0, members // 4, members // 2, members})
    jobs = [(0, part) for part in zip(cuts[:-1], cuts[1:], strict=True)]
    bases, mark = [], [d_mixed[-1]]
    for c in chunks:
        _, g_c, gain_c = inner[c][:3]
        out = normed_output(layout, place, mixed[c], g_c, gain_c, inv, c, out, mark)
        output, gain_grad = out
        mark = [gain_grad]
        if c == CHUNKS - 1 and CHUNKS > 1:
            mark = inner_job(mark, *jobs.pop(0))
            mark = gain_job(mark)
        total = group_total(layout, place, got[c], mark)
        mark = [total]
        bases.append(cross_groups(total, members, context, False))

    def between(c, mark):
        if jobs:
            mark = inner_job(mark, *jobs.pop(0))
        mark = gain_job(mark)
        while c == CHUNKS - 1 and (jobs or steps):
            mark = inner_job(mark, *jobs.pop(0)) if jobs else mark
            mark = gain_job(mark)
        return mark

    gain = (lambda: gain_grad) if regular else None
    later, mark = scatter_back(layout, place, got, bases, context, False, mark, between, gain)
    for c in chunks[1:]:
        mark = inner_job(mark, c, (0, members))
    outer = []
    for group in (early, middle + late):
        if group:
            extra = regular and group != early
            *outer, total_gain = [*outer_gradients(layout, place, k_kept, v_kept, own, later, group, outer, extra), None][:3]
    if not regular:
        total_gain = lax.psum(gain_grad, ("dp", "context"))
    return output[None], dq[0][None], outer[0][None], outer[1][None], total_gain.reshape(features)


def solution(mesh):
    sharded = P("dp", "context", None)
    return jax.shard_map(
        functools.partial(shards, mesh.shape["dp"], mesh.shape["context"]),
        mesh=mesh,
        in_specs=(sharded, sharded, sharded, P(), sharded),
        out_specs=(sharded, sharded, sharded, sharded, P()),
        check_vma=False,
    )
```

```python
import functools

import jax
import jax.numpy as jnp
from jax import lax
from jax.experimental import pallas as pl
from jax.experimental.pallas import tpu as pltpu
from jax.sharding import PartitionSpec as P

HD = 128
EPSILON = 1e-06
BF16 = jnp.bfloat16
F32 = jnp.float32
CHUNKS = 2
MIX_HINTS = (2, 0, 0)
OUTER_HINTS = (2, 0)
SPREAD_HINT = 0
JOB_HINTS = (0, 0, 0, 0)
NORM_HINTS = (0, 0)
VMEM_LIMIT = 14 * 1024 * 1024


def dot(a, b, contract):
    return lax.dot_general(a, b, ((contract[:1], contract[1:]), ((), ())), preferred_element_type=F32)


def divisor(n, choices):
    return next(c for c in choices if n % c == 0)


def lanes(head):
    return slice(head * HD, (head + 1) * HD)


def resident(array):
    return pltpu.with_memory_space_constraint(array, pltpu.VMEM)


def pairs_of(count):
    step = 2 if count % 2 == 0 else 1
    return [range(h, h + step) for h in range(0, count, step)]


def rows_of(head, offset=0):
    return slice(offset + head * HD, offset + (head + 1) * HD)


def span(heads):
    return slice(heads[0] * HD, (heads[-1] + 1) * HD)


def diagonal(blocks):
    if len(blocks) == 1:
        return blocks[0]
    zero = jnp.zeros_like(blocks[0])
    return jnp.concatenate([jnp.concatenate([blocks[0], zero], 1), jnp.concatenate([zero, blocks[1]], 1)], 0)


HBM_WHOLE = pl.BlockSpec(memory_space=pl.ANY)


class Layout:
    def __init__(self, tokens, features, members, chunks):
        self.tokens = tokens
        self.features = features
        self.heads = features // HD
        self.members = members
        self.chunks = chunks
        self.count = self.heads // members // chunks
        self.width = self.count * HD
        self.size = self.count * members * tokens * HD

    def wide(self, chunk, first=0):
        chunks = self.chunks
        return pl.BlockSpec((self.tokens, self.width), lambda k, r: (0, (r[0] ^ (k + first)) * chunks + chunk))

    def columns(self, r, piece, chunk):
        return pl.ds(pl.multiple_of(((r[0] ^ piece) * self.chunks + chunk) * self.width, self.width), self.width)

    def wide_shape(self, kind=BF16):
        return jax.ShapeDtypeStruct((self.tokens, self.features), kind)

    def row_shape(self):
        return jax.ShapeDtypeStruct((1, self.features), F32)

    def kept(self, kind):
        return pltpu.VMEM((self.members, self.tokens, self.width), kind)

    def kept_row(self):
        return pltpu.VMEM((self.members, 1, self.width), F32)

    def narrow(self):
        return pltpu.VMEM((self.tokens, HD), F32)

    def piece(self, extra=0):
        return pltpu.VMEM((self.count * HD + extra, HD), BF16)

    def cut(self):
        return self.tokens // 256 * 256 if self.tokens > 256 and self.tokens % 256 % 16 == 0 else self.tokens

    def weights(self):
        cut, rest = self.cut(), max(self.tokens - self.cut(), 16)
        lead = (self.members, self.count)
        return [pltpu.VMEM((*lead, self.tokens, cut), BF16), pltpu.VMEM((*lead, rest, rest), BF16)]

    def token(self):
        return pltpu.VMEM((8, HD), F32)

    def call(self, name, body, rank, streamed, held, outs, after=(), into=(), macs=0, moved=0, scratch=(), grid=(1,), hint=0):
        whole = pl.BlockSpec(memory_space=pltpu.VMEM)
        unread = pl.BlockSpec(memory_space=pl.ANY)
        operands = [pltpu.with_memory_space_constraint(a, pltpu.HBM) for a in streamed]
        operands += [resident(a) for a in [*held, *after]]
        operands += [pltpu.with_memory_space_constraint(a, memory) for a, _, memory in into]
        first = 1 + len(streamed) + len(held) + len(after)
        used = len(streamed) + len(held)
        skipped = len(after) + len(into)

        def kernel(r, *refs):
            body(r, *refs[:used], *refs[used + skipped :])

        return pl.pallas_call(
            kernel,
            name=name,
            grid_spec=pltpu.PrefetchScalarGridSpec(
                num_scalar_prefetch=1,
                grid=grid,
                in_specs=[unread] * len(streamed) + [whole] * len(held) + [unread] * skipped,
                out_specs=[whole if s is None else s for _, s in outs],
                scratch_shapes=list(scratch),
            ),
            out_shape=[s for s, _ in outs],
            input_output_aliases={first + n: at for n, (_, at, _) in enumerate(into)},
            compiler_params=pltpu.CompilerParams(vmem_limit_bytes=VMEM_LIMIT),
            cost_estimate=pl.CostEstimate(
                flops=int(hint * 1e9) + 1, bytes_accessed=int(hint * 3.6e6) + 1, transcendentals=0
            ),
        )(rank, *operands)


def for_piece(refs, act):
    for k, ref in enumerate(refs):

        @pl.when(pl.program_id(0) == k)
        def _(ref=ref):
            act(ref)


def block_states(layout, rank, keys, values, chunk):
    members = layout.members

    def body(r, k_hbm, v_hbm, k_out, v_out, *refs):
        outs, sems = refs[:members], refs[members]
        copies = []
        for piece in range(members):
            at = layout.columns(r, piece, chunk)
            copies.append(pltpu.make_async_copy(k_hbm.at[:, at], k_out.at[piece], sems.at[0, piece]))
            copies.append(pltpu.make_async_copy(v_hbm.at[:, at], v_out.at[piece], sems.at[1, piece]))
        for copy in copies:
            copy.start()
        for piece in range(members):
            copies[2 * piece].wait()
            copies[2 * piece + 1].wait()
            states = [dot(k_out[piece, :, lanes(h)], v_out[piece, :, lanes(h)], (0, 0)) for h in range(layout.count)]
            for h, state in enumerate(states):
                outs[piece][lanes(h), :] = state.astype(BF16)

    k, v, *states = layout.call(
        "block_states", body, rank, [keys, values], [],
        [(layout.kept(BF16), None)] * 2 + [(layout.piece(), None)] * members,
        macs=layout.size * HD, moved=4 * layout.size, scratch=[pltpu.SemaphoreType.DMA((2, members))],
    )
    return k, v, states


def masked(product):
    rows = lax.broadcasted_iota(jnp.int32, product.shape, 0)
    columns = lax.broadcasted_iota(jnp.int32, product.shape, 1)
    return jnp.where(rows >= columns, product, 0.0).astype(BF16)


def masked_product(a, b, cut):
    blocks = [masked(dot(a, b[:cut], (1, 1)))]
    if cut < a.shape[0]:
        blocks.append(masked(dot(a[cut:], b[cut:], (1, 1))))
    return blocks


def store_product(out, at, blocks, b, cut, add=None):
    rows, columns = at[1:] if len(at) == 3 else at
    lead = at[:-2]
    full = dot(blocks[0], b[:cut], (1, 0))
    full = full if add is None else full + add
    out[(*lead, slice(0, cut), columns)] = full[:cut].astype(out.dtype)
    if len(blocks) > 1:
        out[(*lead, slice(cut, None), columns)] = (full[cut:] + dot(blocks[1], b[cut:], (1, 0))).astype(out.dtype)


def store_turned(out, at, blocks, b, cut):
    lead, columns = at[:-2], at[-1]
    out[(*lead, slice(0, cut), columns)] = dot(blocks[0], b, (0, 0))
    if len(blocks) > 1:
        out[(*lead, slice(cut, None), columns)] = dot(blocks[1], b[cut:], (0, 0))


def within_block(layout, rank, queries, out_grad, gain, keys, values, chunk, after):
    members = layout.members

    def body(r, q_hbm, g_hbm, gain_ref, k_ref, v_ref, q_out, g_out, gain_out, o_ref, *refs):
        w_refs, sems = refs[:-1], refs[-1]
        q_copies, g_copies = [], []
        for piece in range(members):
            at = layout.columns(r, piece, chunk)
            q_copies.append(pltpu.make_async_copy(q_hbm.at[:, at], q_out.at[piece], sems.at[0, piece]))
            g_copies.append(pltpu.make_async_copy(g_hbm.at[:, at], g_out.at[piece], sems.at[1, piece]))
        for copy in q_copies + g_copies:
            copy.start()
        for piece in range(members):
            gain_out[piece] = gain_ref[:, layout.columns(r, piece, chunk)]
            q_copies[piece].wait()
            weights = []
            for h in range(layout.count):
                weights.append(masked_product(q_out[piece, :, lanes(h)], k_ref[piece, :, lanes(h)], layout.cut()))
            for h in range(layout.count):
                for w_ref, block in zip(w_refs, weights[h]):
                    w_ref[piece, h] = block
                store_product(o_ref, (piece, slice(None), lanes(h)), weights[h], v_ref[piece, :, lanes(h)], layout.cut())
        for copy in g_copies:
            copy.wait()

    return layout.call(
        "within_block", body, rank, [queries, out_grad], [gain, keys, values],
        [(layout.kept(BF16), None)] * 2 + [(layout.kept_row(), None), (layout.kept(F32), None)]
        + [(shape, None) for shape in layout.weights()],
        after=after, macs=2 * layout.size * layout.tokens, moved=4 * layout.size, scratch=[pltpu.SemaphoreType.DMA((2, members))],
    )


def mix(layout, rank, kept, prior, jobs, mixed, sums, hint):
    chunks = sorted({c for c, _ in jobs})
    fields = [kept[c][n] for c in chunks for n in (3, 0, 1, 2)]
    states = [prior[c][k][0] for c, k in jobs]
    old = [(n, mixed[c]) for n, c in enumerate(chunks) if c in mixed]

    def body(r, *refs):
        fields_in, refs = refs[: len(fields)], refs[len(fields) :]
        state_refs, refs = refs[: len(jobs)], refs[len(jobs) :]
        before, (*m_refs, square_ref, cross_ref) = refs[: len(sums)], refs[len(sums) :]
        square = before[0][...] if sums else jnp.zeros(square_ref.shape, F32)
        cross = before[1][...] if sums else jnp.zeros(cross_ref.shape, F32)
        for (c, piece), state in zip(jobs, state_refs, strict=True):
            n, offset = chunks.index(c), prior[c][piece][1]
            o_ref, q_ref, g_ref, gain_ref = fields_in[4 * n : 4 * n + 4]
            products = []
            for heads in pairs_of(layout.count):
                block = diagonal([state[rows_of(h, offset), :] for h in heads])
                both = dot(q_ref[piece, :, span(heads)], block, (1, 0))
                products += [both[:, lanes(m)] for m in range(len(heads))]
            for h in range(layout.count):
                at = (piece, slice(None), lanes(h))
                value = o_ref[at] + products[h]
                m_refs[n][at] = value
                square = square + value * value
                cross = cross + gain_ref[piece, :, lanes(h)] * g_ref[at].astype(F32) * value
        square_ref[...] = square
        cross_ref[...] = cross

    *outs, square, cross = layout.call(
        "mix", body, rank, [], [*fields, *states, *sums],
        [(layout.kept(F32), None)] * len(chunks) + [(layout.narrow(), None)] * 2,
        into=[(a, n, pltpu.VMEM) for n, a in old], hint=hint,
    )
    return {**mixed, **dict(zip(chunks, outs, strict=True))}, [square, cross]


def norm_factors(layout, rank, square, cross):
    def body(r, square_ref, cross_ref, inv_ref, factor_ref):
        mean = jnp.sum(square_ref[...], -1, keepdims=True) / layout.features
        inv = lax.rsqrt(mean + EPSILON)
        centered = jnp.sum(cross_ref[...], -1, keepdims=True) / layout.features
        inv_ref[...] = jnp.broadcast_to(inv, inv_ref.shape)
        factor_ref[...] = jnp.broadcast_to(inv * inv * inv * centered, factor_ref.shape)

    return layout.call(
        "norm_factors", body, rank, [], [square, cross], [(layout.narrow(), None)] * 2, moved=layout.tokens * HD * 4
    )


def mixed_gradients(layout, rank, mixed, queries, out_grad, gain, inv, factor):
    def body(r, m_ref, q_ref, g_ref, gain_ref, inv_ref, factor_ref, d_ref, *outs):
        piece = pl.program_id(0)

        def act(out):
            for h in range(layout.count):
                at = (piece, slice(None), lanes(h))
                scaled = gain_ref[piece, :, lanes(h)] * g_ref[at].astype(F32)
                grad = (inv_ref[...] * scaled - m_ref[at] * factor_ref[...]).astype(BF16)
                d_ref[at] = grad
                out[lanes(h), :] = dot(q_ref[at], grad, (0, 0)).astype(BF16)

        for_piece(outs, act)

    d_mixed, *states = layout.call(
        "mixed_gradients", body, rank, [], [mixed, queries, out_grad, gain, inv, factor],
        [(layout.kept(BF16), None)] + [(layout.piece(), None)] * layout.members,
        macs=layout.size * HD, moved=layout.size, grid=(layout.members,),
    )
    return d_mixed, states


def normed_output(layout, rank, mixed, out_grad, gain, inv, chunk, gain_grad, after, hint):
    def body(r, m_ref, g_ref, gain_ref, inv_ref, o_ref, part_ref):
        for piece in range(layout.members):
            for h in range(layout.count):
                here = (piece, slice(None), lanes(h))
                normed = m_ref[here] * inv_ref[...]
                o_ref[here] = (normed * gain_ref[piece, :, lanes(h)]).astype(BF16)
                head = ((r[0] ^ piece) * layout.chunks + chunk) * layout.count + h
                part_ref[pl.ds(head, 1), :] = jnp.sum(g_ref[here].astype(F32) * normed, 0, keepdims=True)

    return layout.call(
        "normed_output", body, rank, [], [mixed, out_grad, gain, inv],
        [(layout.kept(BF16), None), (pltpu.VMEM((layout.heads, HD), F32), None)],
        into=[(a, 1, pltpu.VMEM) for a in gain_grad], after=after, hint=hint,
    )


def inner_gradients(layout, rank, weights, queries, keys, values, d_mixed, prior, chunk, part, own, after, ready=(), stream=(), hint=0):
    first, last = part
    hbm = [(layout.wide_shape(), HBM_WHOLE)] * 2 if ready else []

    def body(r, *refs):
        w_refs, (q_ref, k_ref, v_ref, d_ref, *refs) = refs[: len(weights)], refs[len(weights) :]
        states, refs = refs[: last - first], refs[last - first :]
        ready_refs, (dq_ref, dk_ref, dv_ref, token_ref, *refs) = refs[: len(ready)], refs[len(ready) :]
        hbm_refs, (state, sems) = refs[: len(hbm)], refs[len(hbm) :]
        step = pl.program_id(0)
        piece = step + first
        token_ref[...] = jnp.zeros_like(token_ref)

        def write(n, c, source, at):
            target = hbm_refs[n].at[:, layout.columns(r, at, c)]
            return pltpu.make_async_copy(source.at[at], target, sems.at[n * layout.chunks + c, at])

        def kept_copies(members):
            for (c, _), ref in zip(ready, ready_refs, strict=True):
                for at in range(layout.members):
                    yield write(0, c, ref, at)
            for at in range(members if ready else 0):
                yield write(1, chunk, dq_ref, at)

        @pl.when(step == 0)
        def _():
            for copy in kept_copies(first):
                copy.start()

        for n, (ref, (_, offset)) in enumerate(zip(states, prior[first:last], strict=True)):

            @pl.when(step == n)
            def _(ref=ref, offset=offset):
                state[...] = ref[offset : offset + layout.count * HD, :]

        d_weights, from_prior = [], []
        for h in range(layout.count):
            at = (piece, slice(None), lanes(h))
            d_weights.append(masked_product(d_ref[at], v_ref[at], layout.cut()))
        for heads in pairs_of(layout.count):
            both = dot(d_ref[piece, :, span(heads)], diagonal([state[lanes(h), :] for h in heads]), (1, 1))
            from_prior += [both[:, lanes(n)] for n in range(len(heads))]
        for h in range(layout.count):
            at = (piece, slice(None), lanes(h))
            kept = [w_ref[piece, h] for w_ref in w_refs][: len(d_weights[h])]
            store_product(dq_ref, at[1:] if stream else at, d_weights[h], k_ref[at], layout.cut(), from_prior[h])
            store_turned(dk_ref, at, d_weights[h], q_ref[at], layout.cut())
            store_turned(dv_ref, at, kept, d_ref[at], layout.cut())
        if ready:
            write(1, chunk, dq_ref, piece).start()

        @pl.when(step == last - first - 1)
        def _():
            for copy in kept_copies(layout.members):
                copy.wait()

    dq = (layout.wide_shape(), layout.wide(chunk, first)) if stream else (layout.kept(BF16), None)
    return layout.call(
        "inner_gradients", body, rank, [],
        [*weights, queries, keys, values, d_mixed, *[a for a, _ in prior[first:last]], *[a for _, a in ready]],
        [dq, (layout.kept(F32), None), (layout.kept(F32), None), (layout.token(), None)] + hbm,
        into=[(a, n, pltpu.VMEM) for n, a in enumerate(own)] + [(a, 0, pltpu.HBM) for a in stream], after=after,
        scratch=[pltpu.VMEM((layout.count * HD, HD), BF16), pltpu.SemaphoreType.DMA((2 * layout.chunks, layout.members))],
        grid=(last - first,), hint=hint,
    )


def pairwise(terms):
    while len(terms) > 1:
        terms = [a + b for a, b in zip(terms[::2], terms[1::2], strict=True)]
    return terms[0]


def outer_gradients(layout, rank, keys, values, own, later, jobs, into, extra, hint):
    chunks = sorted({c for c, _ in jobs})
    fields = [a for c in chunks for a in (keys[c], values[c], *own[c][1:])]
    states = [later[c][k][0] for c, k in jobs]
    count, heads_all = len(jobs), layout.heads
    gain_out = [(jax.ShapeDtypeStruct((heads_all, HD), F32), HBM_WHOLE)] if extra else []

    def body(r, *refs):
        fields_in, refs = refs[: len(fields)], refs[len(fields) :]
        state_refs, (dk_hbm, dv_hbm, *refs) = refs[:count], refs[count:]
        gain_hbm, (dk_buffer, dv_buffer, gain_buffer, sems) = refs[: len(gain_out)], refs[len(gain_out) :]
        copies = []
        if extra:
            parts = []
            for _, n in sorted((piece, n) for n, (c, piece) in enumerate(jobs) if c == chunks[-1]):
                rows = state_refs[n][-2 * heads_all :, :].astype(F32)
                parts.append(rows[:heads_all] + rows[heads_all:])
            gain_buffer[...] = pairwise(parts)
            copies.append(pltpu.make_async_copy(gain_buffer, gain_hbm[0], sems.at[2, 0]))
            copies[-1].start()
        for n, ((c, piece), state) in enumerate(zip(jobs, state_refs, strict=True)):
            at, offset = layout.columns(r, piece, c), later[c][piece][1]
            k_ref, v_ref, dki_ref, dvi_ref = fields_in[4 * chunks.index(c) : 4 * chunks.index(c) + 4]
            sums = []
            for heads in pairs_of(layout.count):
                here = (piece, slice(None), span(heads))
                block = diagonal([state[rows_of(h, offset), :] for h in heads])
                sums.append((heads, here, dot(v_ref[here], block, (1, 1)), dot(k_ref[here], block, (1, 0))))
            for heads, here, dk, dv in sums:
                dk_buffer[n, :, span(heads)] = (dki_ref[here] + dk).astype(BF16)
                dv_buffer[n, :, span(heads)] = (dvi_ref[here] + dv).astype(BF16)
            copies.append(pltpu.make_async_copy(dk_buffer.at[n], dk_hbm.at[:, at], sems.at[0, n]))
            copies.append(pltpu.make_async_copy(dv_buffer.at[n], dv_hbm.at[:, at], sems.at[1, n]))
            copies[-2].start()
            copies[-1].start()
        for copy in copies:
            copy.wait()

    return layout.call(
        "outer_gradients", body, rank, [], [*fields, *states],
        [(layout.wide_shape(), HBM_WHOLE)] * 2 + gain_out,
        into=[(a, n, pltpu.HBM) for n, a in enumerate(into)],
        macs=2 * layout.size * HD, moved=4 * layout.size, hint=hint,
        scratch=[pltpu.VMEM((count, layout.tokens, layout.width), BF16)] * 2
        + [pltpu.VMEM((heads_all, HD), F32), pltpu.SemaphoreType.DMA((3, count))],
    )


def swap(array, axis, size, k):
    return lax.ppermute(array, axis, [(c, c ^ k) for c in range(size)])


def gather_home(pieces, context):
    order = range(len(pieces) - 1, 0, -1)
    got = {k: swap(pieces[k], "context", context, k) for k in order}
    return [pieces[0]] + [got[k] for k in range(1, len(pieces))]


def group_total(layout, rank, got, after):
    def body(r, *refs):
        *gots, total = refs
        total[...] = sum(g[...].astype(F32) for g in gots).astype(BF16)

    return layout.call(
        "group_total", body, rank, [], got, [(layout.piece(), None)], after=after, moved=layout.count * HD * HD * 10
    )[0]


def cross_groups(total, members, context, forward):
    bases = []
    for far in range(1, context // members):
        hop = far * members
        up = [(c, c + hop) for c in range(context - hop)]
        bases.append(lax.ppermute(total, "context", up if forward else [(b, a) for a, b in up]))
    return bases


def spread(layout, rank, got, bases, forward, after, joined=(), gain=(), hint=0):
    members, heads_all = layout.members, layout.heads
    extra = 2 * heads_all * len(gain)
    shift = layout.count * HD * len(joined)

    def body(r, *refs):
        gots, rest = refs[:members], refs[members:]
        lows, rest = rest[: len(bases)], rest[len(bases) :]
        joined_refs, rest = rest[: len(joined)], rest[len(joined) :]
        gains, outs = rest[: len(gain)], rest[len(gain) :]
        for n, ref in enumerate(joined_refs):
            outs[-1][n * layout.count * HD : (n + 1) * layout.count * HD, :] = ref[...]
        for h in range(layout.count):
            held = [g[rows_of(h), :].astype(F32) for g in gots]
            base = sum((low[rows_of(h), :].astype(F32) for low in lows), jnp.zeros((HD, HD), F32))
            for k in range(members):
                part = base
                for j in range(members):
                    if j != k:
                        one, other = r[0] ^ j, r[0] ^ k
                        ahead = one < other if forward else one > other
                        part = part + held[j] * ahead.astype(F32)
                outs[k][rows_of(h, shift if k == members - 1 else 0), :] = part.astype(BF16)
        for ref in gains:
            high = ref[...].astype(BF16)
            low = (ref[...] - high.astype(F32)).astype(BF16)
            for out in outs:
                rows = out.shape[0]
                out[rows - 2 * heads_all : rows - heads_all, :] = high
                out[rows - heads_all : rows, :] = low

    return layout.call(
        "spread", body, rank, [], [*got, *bases, *joined, *gain],
        [(layout.piece(extra), None)] * (members - 1) + [(layout.piece(extra + shift), None)], after=after,
        hint=hint,
    )


def scatter_back(layout, rank, got, bases, context, forward, mark, between, gain=None, hint=0):
    far, joined, pieces = layout.members - 1, [], []
    for c in range(layout.chunks):
        final = c == layout.chunks - 1
        mark = between(c, mark)
        rows = [gain()] if final and gain else []
        outs = spread(layout, rank, got[c], bases[c], forward, mark, joined if final else [], rows, hint)
        mark = [outs[0]]
        joined.append(outs[far])
        order = range(far if final else far - 1, 0, -1)
        moved = {k: swap(outs[k], "context", context, k) for k in order}
        pieces.append([(moved.get(k, outs[k]), 0) for k in range(layout.members)])
    if far:
        last = pieces[-1][far][0]
        for c, chunk in enumerate(pieces):
            chunk[far] = (last, c * layout.count * HD)
    return pieces, mark


def xor_steps(axis, size, stride):
    steps = []
    while stride < size:
        steps.append((axis, size, stride))
        stride *= 2
    return steps


def added(layout, rank, one, other, after):
    def body(r, one_ref, other_ref, out_ref):
        out_ref[...] = one_ref[...] + other_ref[...]

    return layout.call(
        "gain_sum", body, rank, [], [one, other], [(pltpu.VMEM(one.shape, F32), None)], after=after, moved=one.size * 12
    )[0]


def shards(dp, context, queries, keys, values, gain, out_grad):
    tokens, features = queries.shape[1:]
    members = divisor(context, (4, 2, 1))
    layout = Layout(tokens, features, members, CHUNKS)
    chunks = range(CHUNKS)
    place = (lax.axis_index("context") % members).astype(jnp.int32).reshape(1)
    q, k, v, g = (array[0] for array in (queries, keys, values, out_grad))
    gain_row = gain.reshape(1, features)

    k_kept, v_kept, got = [], [], []
    for c in chunks:
        k_c, v_c, states = block_states(layout, place, k, v, c)
        k_kept.append(k_c)
        v_kept.append(v_c)
        got.append(gather_home(states, context))
    inner, bases, mark = [], [], []
    for c in chunks:
        total = group_total(layout, place, got[c], mark)
        bases.append(cross_groups(total, members, context, True))
        inner.append(within_block(layout, place, q, g, gain_row, k_kept[c], v_kept[c], c, [total]))
        mark = [inner[c][3]]
    prior, mark = scatter_back(layout, place, got, bases, context, True, mark, lambda c, mark: mark)
    far = members - 1
    early = [(c, k) for c in chunks[:-1] for k in range(far)]
    middle = [(CHUNKS - 1, k) for k in range(far)]
    late = [(c, far) for c in chunks]
    mixed, sums = {}, []
    for group, hint in zip((early, middle, late), MIX_HINTS, strict=True):
        if group:
            mixed, sums = mix(layout, place, inner, prior, group, mixed, sums, hint)
    inv, factor = norm_factors(layout, place, *sums)

    d_mixed, got = [], []
    for c in chunks:
        q_c, g_c, gain_c = inner[c][:3]
        d_c, states = mixed_gradients(layout, place, mixed[c], q_c, g_c, gain_c, inv, factor)
        d_mixed.append(d_c)
        got.append(gather_home(states, context))

    normed, own, gain_grad = {}, [[] for _ in chunks], []
    regular = dp & (dp - 1) == 0 and context & (context - 1) == 0
    steps = xor_steps("dp", dp, 1) + xor_steps("context", context, members) if regular else []

    def inner_job(mark, c, part, ready=(), stream=(), hint=0):
        result = inner_gradients(
            layout, place, inner[c][4:], inner[c][0], k_kept[c], v_kept[c], d_mixed[c], prior[c], c, part, own[c], mark, ready, stream, hint
        )
        *own[c], token = result[:4]
        return [token], result[4:]

    def gain_job(mark):
        nonlocal gain_grad
        if not steps:
            return mark
        axis, size, stride = steps.pop(0)
        gain_grad = [added(layout, place, *gain_grad, swap(*gain_grad, axis, size, stride), mark)]
        return gain_grad

    cuts = sorted({0, members // 4, members // 2, members})
    jobs = [(0, part) for part in zip(cuts[:-1], cuts[1:], strict=True)]
    bases, mark = [], [d_mixed[-1]]
    for c in chunks:
        _, g_c, gain_c = inner[c][:3]
        normed[c], *gain_grad = normed_output(layout, place, mixed[c], g_c, gain_c, inv, c, gain_grad, mark, NORM_HINTS[c])
        mark = gain_grad
        if c == CHUNKS - 1:
            mark, _ = inner_job(mark, *jobs.pop(0), hint=JOB_HINTS[0])
            mark = gain_job(mark)
        total = group_total(layout, place, got[c], mark)
        mark = [total]
        bases.append(cross_groups(total, members, context, False))

    written = []

    def between(c, mark):
        nonlocal written
        if jobs:
            job = jobs.pop(0)
            mark, written = inner_job(mark, *job, () if jobs else [*normed.items()], hint=JOB_HINTS[1 + c])
        mark = gain_job(mark)
        while c == CHUNKS - 1 and steps:
            mark = gain_job(mark)
        return mark

    gain = (lambda: gain_grad[0]) if regular else None
    later, mark = scatter_back(layout, place, got, bases, context, False, mark, between, gain, SPREAD_HINT)
    for c in chunks[1:]:
        output, query_grad = written
        mark, _ = inner_job(mark, c, (0, members), (), [query_grad], JOB_HINTS[3])
        written = [output, own[c][0]]
    output, query_grad = written
    outer = []
    for group, hint in zip((early, middle + late), OUTER_HINTS, strict=True):
        if group:
            extra = regular and group != early
            *outer, total_gain = [*outer_gradients(layout, place, k_kept, v_kept, own, later, group, outer, extra, hint), None][:3]
    if not regular:
        total_gain = lax.psum(gain_grad[0], ("dp", "context"))
    return output[None], query_grad[None], outer[0][None], outer[1][None], total_gain.reshape(features)


def solution(mesh):
    sharded = P("dp", "context", None)
    return jax.shard_map(
        functools.partial(shards, mesh.shape["dp"], mesh.shape["context"]),
        mesh=mesh,
        in_specs=(sharded, sharded, sharded, P(), sharded),
        out_specs=(sharded, sharded, sharded, sharded, P()),
        check_vma=False,
    )
```

```python
import functools

import jax
import jax.numpy as jnp
from jax import lax
from jax.experimental import pallas as pl
from jax.experimental.pallas import tpu as pltpu
from jax.sharding import PartitionSpec as P

HD = 128
EPSILON = 1e-06
BF16 = jnp.bfloat16
F32 = jnp.float32
CHUNKS = 2
MIX_HINTS = (10, 10, 10)
OUTER_HINT = 2
SPREAD_HINT = 0
VMEM_LIMIT = 14 * 1024 * 1024


def dot(a, b, contract):
    return lax.dot_general(a, b, ((contract[:1], contract[1:]), ((), ())), preferred_element_type=F32)


def divisor(n, choices):
    return next(c for c in choices if n % c == 0)


def lanes(head):
    return slice(head * HD, (head + 1) * HD)


def resident(array):
    return pltpu.with_memory_space_constraint(array, pltpu.VMEM)


def pairs_of(count):
    step = 2 if count % 2 == 0 else 1
    return [range(h, h + step) for h in range(0, count, step)]


def rows_of(head, offset=0):
    return slice(offset + head * HD, offset + (head + 1) * HD)


def span(heads):
    return slice(heads[0] * HD, (heads[-1] + 1) * HD)


def diagonal(blocks):
    if len(blocks) == 1:
        return blocks[0]
    zero = jnp.zeros_like(blocks[0])
    return jnp.concatenate([jnp.concatenate([blocks[0], zero], 1), jnp.concatenate([zero, blocks[1]], 1)], 0)


HBM_WHOLE = pl.BlockSpec(memory_space=pl.ANY)


class Layout:
    def __init__(self, tokens, features, members, chunks):
        self.tokens = tokens
        self.features = features
        self.heads = features // HD
        self.members = members
        self.chunks = chunks
        self.count = self.heads // members // chunks
        self.width = self.count * HD
        self.size = self.count * members * tokens * HD

    def wide(self, chunk, first=0):
        chunks = self.chunks
        return pl.BlockSpec((self.tokens, self.width), lambda k, r: (0, (r[0] ^ (k + first)) * chunks + chunk))

    def columns(self, r, piece, chunk):
        return pl.ds(pl.multiple_of(((r[0] ^ piece) * self.chunks + chunk) * self.width, self.width), self.width)

    def wide_shape(self, kind=BF16):
        return jax.ShapeDtypeStruct((self.tokens, self.features), kind)

    def row_shape(self):
        return jax.ShapeDtypeStruct((1, self.features), F32)

    def kept(self, kind):
        return pltpu.VMEM((self.members, self.tokens, self.width), kind)

    def kept_row(self):
        return pltpu.VMEM((self.members, 1, self.width), F32)

    def narrow(self):
        return pltpu.VMEM((self.tokens, HD), F32)

    def piece(self, extra=0):
        return pltpu.VMEM((self.count * HD + extra, HD), BF16)

    def cut(self):
        return self.tokens // 256 * 256 if self.tokens > 256 and self.tokens % 256 % 16 == 0 else self.tokens

    def weights(self):
        cut, rest = self.cut(), max(self.tokens - self.cut(), 16)
        lead = (self.members, self.count)
        return [pltpu.VMEM((*lead, self.tokens, cut), BF16), pltpu.VMEM((*lead, rest, rest), BF16)]

    def token(self):
        return pltpu.VMEM((8, HD), F32)

    def call(self, name, body, rank, streamed, held, outs, after=(), into=(), macs=0, moved=0, scratch=(), grid=(1,), hint=0):
        whole = pl.BlockSpec(memory_space=pltpu.VMEM)
        unread = pl.BlockSpec(memory_space=pl.ANY)
        operands = [pltpu.with_memory_space_constraint(a, pltpu.HBM) for a in streamed]
        operands += [resident(a) for a in [*held, *after]]
        operands += [pltpu.with_memory_space_constraint(a, memory) for a, _, memory in into]
        first = 1 + len(streamed) + len(held) + len(after)
        used = len(streamed) + len(held)
        skipped = len(after) + len(into)

        def kernel(r, *refs):
            body(r, *refs[:used], *refs[used + skipped :])

        return pl.pallas_call(
            kernel,
            name=name,
            grid_spec=pltpu.PrefetchScalarGridSpec(
                num_scalar_prefetch=1,
                grid=grid,
                in_specs=[unread] * len(streamed) + [whole] * len(held) + [unread] * skipped,
                out_specs=[whole if s is None else s for _, s in outs],
                scratch_shapes=list(scratch),
            ),
            out_shape=[s for s, _ in outs],
            input_output_aliases={first + n: at for n, (_, at, _) in enumerate(into)},
            compiler_params=pltpu.CompilerParams(vmem_limit_bytes=VMEM_LIMIT),
            cost_estimate=pl.CostEstimate(
                flops=int(hint * 1e9) + 1, bytes_accessed=int(hint * 3.6e6) + 1, transcendentals=0
            ),
        )(rank, *operands)


def for_piece(refs, act):
    for k, ref in enumerate(refs):

        @pl.when(pl.program_id(0) == k)
        def _(ref=ref):
            act(ref)


def block_states(layout, rank, keys, values, chunk):
    members = layout.members

    def body(r, k_hbm, v_hbm, k_out, v_out, *refs):
        outs, sems = refs[:members], refs[members]
        copies = []
        for piece in range(members):
            at = layout.columns(r, piece, chunk)
            copies.append(pltpu.make_async_copy(k_hbm.at[:, at], k_out.at[piece], sems.at[0, piece]))
            copies.append(pltpu.make_async_copy(v_hbm.at[:, at], v_out.at[piece], sems.at[1, piece]))
        for copy in copies:
            copy.start()
        for piece in range(members):
            copies[2 * piece].wait()
            copies[2 * piece + 1].wait()
            states = [dot(k_out[piece, :, lanes(h)], v_out[piece, :, lanes(h)], (0, 0)) for h in range(layout.count)]
            for h, state in enumerate(states):
                outs[piece][lanes(h), :] = state.astype(BF16)

    k, v, *states = layout.call(
        "block_states", body, rank, [keys, values], [],
        [(layout.kept(BF16), None)] * 2 + [(layout.piece(), None)] * members,
        macs=layout.size * HD, moved=4 * layout.size, scratch=[pltpu.SemaphoreType.DMA((2, members))],
    )
    return k, v, states


def masked(product):
    rows = lax.broadcasted_iota(jnp.int32, product.shape, 0)
    columns = lax.broadcasted_iota(jnp.int32, product.shape, 1)
    return jnp.where(rows >= columns, product, 0.0).astype(BF16)


def masked_product(a, b, cut):
    blocks = [masked(dot(a, b[:cut], (1, 1)))]
    if cut < a.shape[0]:
        blocks.append(masked(dot(a[cut:], b[cut:], (1, 1))))
    return blocks


def store_product(out, at, blocks, b, cut, add=None):
    rows, columns = at[1:] if len(at) == 3 else at
    lead = at[:-2]
    full = dot(blocks[0], b[:cut], (1, 0))
    full = full if add is None else full + add
    out[(*lead, slice(0, cut), columns)] = full[:cut].astype(out.dtype)
    if len(blocks) > 1:
        out[(*lead, slice(cut, None), columns)] = (full[cut:] + dot(blocks[1], b[cut:], (1, 0))).astype(out.dtype)


def store_turned(out, at, blocks, b, cut):
    lead, columns = at[:-2], at[-1]
    out[(*lead, slice(0, cut), columns)] = dot(blocks[0], b, (0, 0))
    if len(blocks) > 1:
        out[(*lead, slice(cut, None), columns)] = dot(blocks[1], b[cut:], (0, 0))


def within_block(layout, rank, queries, out_grad, gain, keys, values, chunk, after):
    members = layout.members

    def body(r, q_hbm, g_hbm, gain_ref, k_ref, v_ref, q_out, g_out, gain_out, o_ref, *refs):
        w_refs, sems = refs[:-1], refs[-1]
        q_copies, g_copies = [], []
        for piece in range(members):
            at = layout.columns(r, piece, chunk)
            q_copies.append(pltpu.make_async_copy(q_hbm.at[:, at], q_out.at[piece], sems.at[0, piece]))
            g_copies.append(pltpu.make_async_copy(g_hbm.at[:, at], g_out.at[piece], sems.at[1, piece]))
        for copy in q_copies + g_copies:
            copy.start()
        for piece in range(members):
            gain_out[piece] = gain_ref[:, layout.columns(r, piece, chunk)]
            q_copies[piece].wait()
            weights = []
            for h in range(layout.count):
                weights.append(masked_product(q_out[piece, :, lanes(h)], k_ref[piece, :, lanes(h)], layout.cut()))
            for h in range(layout.count):
                for w_ref, block in zip(w_refs, weights[h]):
                    w_ref[piece, h] = block
                store_product(o_ref, (piece, slice(None), lanes(h)), weights[h], v_ref[piece, :, lanes(h)], layout.cut())
        for copy in g_copies:
            copy.wait()

    return layout.call(
        "within_block", body, rank, [queries, out_grad], [gain, keys, values],
        [(layout.kept(BF16), None)] * 2 + [(layout.kept_row(), None), (layout.kept(F32), None)]
        + [(shape, None) for shape in layout.weights()],
        after=after, macs=2 * layout.size * layout.tokens, moved=4 * layout.size, scratch=[pltpu.SemaphoreType.DMA((2, members))],
    )


def mix(layout, rank, kept, prior, jobs, mixed, sums, hint):
    chunks = sorted({c for c, _ in jobs})
    fields = [kept[c][n] for c in chunks for n in (3, 0, 1, 2)]
    states = [prior[c][k][0] for c, k in jobs]
    old = [(n, mixed[c]) for n, c in enumerate(chunks) if c in mixed]

    def body(r, *refs):
        fields_in, refs = refs[: len(fields)], refs[len(fields) :]
        state_refs, refs = refs[: len(jobs)], refs[len(jobs) :]
        before, (*m_refs, square_ref, cross_ref) = refs[: len(sums)], refs[len(sums) :]
        square = before[0][...] if sums else jnp.zeros(square_ref.shape, F32)
        cross = before[1][...] if sums else jnp.zeros(cross_ref.shape, F32)
        for (c, piece), state in zip(jobs, state_refs, strict=True):
            n, offset = chunks.index(c), prior[c][piece][1]
            o_ref, q_ref, g_ref, gain_ref = fields_in[4 * n : 4 * n + 4]
            products = []
            for heads in pairs_of(layout.count):
                block = diagonal([state[rows_of(h, offset), :] for h in heads])
                both = dot(q_ref[piece, :, span(heads)], block, (1, 0))
                products += [both[:, lanes(m)] for m in range(len(heads))]
            for h in range(layout.count):
                at = (piece, slice(None), lanes(h))
                value = o_ref[at] + products[h]
                m_refs[n][at] = value
                square = square + value * value
                cross = cross + gain_ref[piece, :, lanes(h)] * g_ref[at].astype(F32) * value
        square_ref[...] = square
        cross_ref[...] = cross

    *outs, square, cross = layout.call(
        "mix", body, rank, [], [*fields, *states, *sums],
        [(layout.kept(F32), None)] * len(chunks) + [(layout.narrow(), None)] * 2,
        into=[(a, n, pltpu.VMEM) for n, a in old], hint=hint,
    )
    return {**mixed, **dict(zip(chunks, outs, strict=True))}, [square, cross]


def norm_factors(layout, rank, square, cross):
    def body(r, square_ref, cross_ref, inv_ref, factor_ref):
        mean = jnp.sum(square_ref[...], -1, keepdims=True) / layout.features
        inv = lax.rsqrt(mean + EPSILON)
        centered = jnp.sum(cross_ref[...], -1, keepdims=True) / layout.features
        inv_ref[...] = jnp.broadcast_to(inv, inv_ref.shape)
        factor_ref[...] = jnp.broadcast_to(inv * inv * inv * centered, factor_ref.shape)

    return layout.call(
        "norm_factors", body, rank, [], [square, cross], [(layout.narrow(), None)] * 2, moved=layout.tokens * HD * 4
    )


def mixed_gradients(layout, rank, mixed, queries, out_grad, gain, inv, factor):
    def body(r, m_ref, q_ref, g_ref, gain_ref, inv_ref, factor_ref, d_ref, *outs):
        piece = pl.program_id(0)

        def act(out):
            for h in range(layout.count):
                at = (piece, slice(None), lanes(h))
                scaled = gain_ref[piece, :, lanes(h)] * g_ref[at].astype(F32)
                grad = (inv_ref[...] * scaled - m_ref[at] * factor_ref[...]).astype(BF16)
                d_ref[at] = grad
                out[lanes(h), :] = dot(q_ref[at], grad, (0, 0)).astype(BF16)

        for_piece(outs, act)

    d_mixed, *states = layout.call(
        "mixed_gradients", body, rank, [], [mixed, queries, out_grad, gain, inv, factor],
        [(layout.kept(BF16), None)] + [(layout.piece(), None)] * layout.members,
        macs=layout.size * HD, moved=layout.size, grid=(layout.members,),
    )
    return d_mixed, states


def normed_output(layout, rank, mixed, out_grad, gain, inv, chunk, gain_grad, after):
    def body(r, m_ref, g_ref, gain_ref, inv_ref, o_ref, part_ref):
        for piece in range(layout.members):
            for h in range(layout.count):
                here = (piece, slice(None), lanes(h))
                normed = m_ref[here] * inv_ref[...]
                o_ref[here] = (normed * gain_ref[piece, :, lanes(h)]).astype(BF16)
                head = ((r[0] ^ piece) * layout.chunks + chunk) * layout.count + h
                part_ref[pl.ds(head, 1), :] = jnp.sum(g_ref[here].astype(F32) * normed, 0, keepdims=True)

    return layout.call(
        "normed_output", body, rank, [], [mixed, out_grad, gain, inv],
        [(layout.kept(BF16), None), (pltpu.VMEM((layout.heads, HD), F32), None)],
        into=[(a, 1, pltpu.VMEM) for a in gain_grad], after=after,
    )


def inner_gradients(
    layout, rank, weights, queries, keys, values, d_mixed, prior, chunk, part, own, after, ready=(), others=(), also=(), hint=0
):
    first, last = part
    targets = ([0] if ready else []) + ([1] if others else []) + ([2, 3] if also else [])
    hbm = [(layout.wide_shape(), HBM_WHOLE)] * len(targets)
    lists = [*((0, c, a) for c, a in ready), *((1, c, a) for c, a in others)]
    extra = max(len(also) - 4, 0)

    def body(r, *refs):
        w_refs, (q_ref, k_ref, v_ref, d_ref, *refs) = refs[: len(weights)], refs[len(weights) :]
        states, refs = refs[: last - first], refs[last - first :]
        list_refs, refs = refs[: len(lists)], refs[len(lists) :]
        also_refs, (dq_ref, dk_ref, dv_ref, token_ref, *refs) = refs[: len(also)], refs[len(also) :]
        hbm_refs, (state, dk_buffer, dv_buffer, sems) = dict(zip(targets, refs)), refs[len(hbm) :]
        step = pl.program_id(0)
        piece = step + first
        token_ref[...] = jnp.zeros_like(token_ref)

        def write(n, c, source, at):
            target = hbm_refs[n].at[:, layout.columns(r, at, c)]
            return pltpu.make_async_copy(source.at[at], target, sems.at[n * layout.chunks + c, at])

        def list_copies():
            for (n, c, _), ref in zip(lists, list_refs, strict=True):
                for at in range(layout.members):
                    yield write(n, c, ref, at)

        def outer_copies(at):
            return [write(n, 0, ref, at) for n, ref in ((2, dk_buffer), (3, dv_buffer))]

        @pl.when(step == 0)
        def _():
            for copy in list_copies():
                copy.start()

        for n, (ref, (_, offset)) in enumerate(zip(states, prior[first:last], strict=True)):

            @pl.when(step == n)
            def _(ref=ref, offset=offset):
                state[...] = ref[offset : offset + layout.count * HD, :]

        for n in range(extra):

            @pl.when(step == n)
            def _(n=n):
                store_outer(layout, also_refs[:4], also_refs[4 + n], 0, n, dk_buffer, dv_buffer, n)
                for copy in outer_copies(n):
                    copy.start()

        d_weights, from_prior = [], []
        for h in range(layout.count):
            at = (piece, slice(None), lanes(h))
            d_weights.append(masked_product(d_ref[at], v_ref[at], layout.cut()))
        for heads in pairs_of(layout.count):
            both = dot(d_ref[piece, :, span(heads)], diagonal([state[lanes(h), :] for h in heads]), (1, 1))
            from_prior += [both[:, lanes(n)] for n in range(len(heads))]
        for h in range(layout.count):
            at = (piece, slice(None), lanes(h))
            kept = [w_ref[piece, h] for w_ref in w_refs][: len(d_weights[h])]
            store_product(dq_ref, at, d_weights[h], k_ref[at], layout.cut(), from_prior[h])
            store_turned(dk_ref, at, d_weights[h], q_ref[at], layout.cut())
            store_turned(dv_ref, at, kept, d_ref[at], layout.cut())
        if others:

            @pl.when(step < last - first - 1)
            def _():
                write(1, chunk, dq_ref, piece).start()

        @pl.when(step == last - first - 1)
        def _():
            for copy in list_copies():
                copy.wait()
            for at in range(first, last - 1 if others else first):
                write(1, chunk, dq_ref, at).wait()
            for n in range(extra):
                for copy in outer_copies(n):
                    copy.wait()

    buffer = pltpu.VMEM((max(extra, 1), layout.tokens, layout.width), BF16)
    return layout.call(
        "inner_gradients", body, rank, [],
        [*weights, queries, keys, values, d_mixed, *[a for a, _ in prior[first:last]], *[a for _, _, a in lists], *also],
        [(layout.kept(BF16), None), (layout.kept(F32), None), (layout.kept(F32), None), (layout.token(), None)] + hbm,
        into=[(a, n, pltpu.VMEM) for n, a in enumerate(own)], after=after, hint=hint,
        scratch=[
            pltpu.VMEM((layout.count * HD, HD), BF16), buffer, buffer,
            pltpu.SemaphoreType.DMA((4 * layout.chunks, layout.members)),
        ],
        grid=(last - first,),
    )


def store_outer(layout, fields, state, offset, piece, dk_buffer, dv_buffer, slot):
    k_ref, v_ref, dki_ref, dvi_ref = fields
    sums = []
    for heads in pairs_of(layout.count):
        here = (piece, slice(None), span(heads))
        block = diagonal([state[rows_of(h, offset), :] for h in heads])
        sums.append((heads, here, dot(v_ref[here], block, (1, 1)), dot(k_ref[here], block, (1, 0))))
    for heads, here, dk, dv in sums:
        dk_buffer[slot, :, span(heads)] = (dki_ref[here] + dk).astype(BF16)
        dv_buffer[slot, :, span(heads)] = (dvi_ref[here] + dv).astype(BF16)


def pairwise(terms):
    while len(terms) > 1:
        terms = [a + b for a, b in zip(terms[::2], terms[1::2], strict=True)]
    return terms[0]


def outer_gradients(layout, rank, keys, values, own, later, jobs, into, extra, queries, query_grad):
    chunks = sorted({c for c, _ in jobs})
    fields = [a for c in chunks for a in (keys[c], values[c], *own[c][1:])]
    states = [later[c][k][0] for c, k in jobs]
    count, heads_all = len(jobs), layout.heads
    gain_out = [(jax.ShapeDtypeStruct((heads_all, HD), F32), HBM_WHOLE)] if extra else []

    def body(r, *refs):
        fields_in, refs = refs[: len(fields)], refs[len(fields) :]
        state_refs, (q_ref, dk_hbm, dv_hbm, dq_hbm, *refs) = refs[:count], refs[count:]
        gain_hbm, (dk_buffer, dv_buffer, gain_buffer, sems) = refs[: len(gain_out)], refs[len(gain_out) :]
        at = layout.columns(r, layout.members - 1, layout.chunks - 1)
        copies = [pltpu.make_async_copy(q_ref.at[layout.members - 1], dq_hbm.at[:, at], sems.at[3, 0])]
        copies[0].start()
        if extra:
            parts = []
            for _, n in sorted((piece, n) for n, (c, piece) in enumerate(jobs) if c == chunks[-1]):
                rows = state_refs[n][-2 * heads_all :, :].astype(F32)
                parts.append(rows[:heads_all] + rows[heads_all:])
            gain_buffer[...] = pairwise(parts)
            copies.append(pltpu.make_async_copy(gain_buffer, gain_hbm[0], sems.at[2, 0]))
            copies[-1].start()
        for n, ((c, piece), state) in enumerate(zip(jobs, state_refs, strict=True)):
            at, offset = layout.columns(r, piece, c), later[c][piece][1]
            here = 4 * chunks.index(c)
            store_outer(layout, fields_in[here : here + 4], state, offset, piece, dk_buffer, dv_buffer, n)
            copies.append(pltpu.make_async_copy(dk_buffer.at[n], dk_hbm.at[:, at], sems.at[0, n]))
            copies.append(pltpu.make_async_copy(dv_buffer.at[n], dv_hbm.at[:, at], sems.at[1, n]))
            copies[-2].start()
            copies[-1].start()
        for copy in copies:
            copy.wait()

    return layout.call(
        "outer_gradients", body, rank, [], [*fields, *states, queries],
        [(layout.wide_shape(), HBM_WHOLE)] * 3 + gain_out,
        into=[(a, n, pltpu.HBM) for n, a in enumerate(into)] + [(query_grad, 2, pltpu.HBM)],
        scratch=[pltpu.VMEM((count, layout.tokens, layout.width), BF16)] * 2
        + [pltpu.VMEM((heads_all, HD), F32), pltpu.SemaphoreType.DMA((4, count))],
    )


def swap(array, axis, size, k):
    return lax.ppermute(array, axis, [(c, c ^ k) for c in range(size)])


def gather_home(pieces, context):
    order = range(len(pieces) - 1, 0, -1)
    got = {k: swap(pieces[k], "context", context, k) for k in order}
    return [pieces[0]] + [got[k] for k in range(1, len(pieces))]


def group_total(layout, rank, got, after):
    def body(r, *refs):
        *gots, total = refs
        total[...] = sum(g[...].astype(F32) for g in gots).astype(BF16)

    return layout.call(
        "group_total", body, rank, [], got, [(layout.piece(), None)], after=after, moved=layout.count * HD * HD * 10
    )[0]


def cross_groups(total, members, context, forward):
    bases = []
    for far in range(1, context // members):
        hop = far * members
        up = [(c, c + hop) for c in range(context - hop)]
        bases.append(lax.ppermute(total, "context", up if forward else [(b, a) for a, b in up]))
    return bases


def spread(layout, rank, got, bases, forward, after, joined=(), gain=(), hint=0):
    members, heads_all = layout.members, layout.heads
    extra = 2 * heads_all * len(gain)
    shift = layout.count * HD * len(joined)

    def body(r, *refs):
        gots, rest = refs[:members], refs[members:]
        lows, rest = rest[: len(bases)], rest[len(bases) :]
        joined_refs, rest = rest[: len(joined)], rest[len(joined) :]
        gains, outs = rest[: len(gain)], rest[len(gain) :]
        for n, ref in enumerate(joined_refs):
            outs[-1][n * layout.count * HD : (n + 1) * layout.count * HD, :] = ref[...]
        for h in range(layout.count):
            held = [g[rows_of(h), :].astype(F32) for g in gots]
            base = sum((low[rows_of(h), :].astype(F32) for low in lows), jnp.zeros((HD, HD), F32))
            for k in range(members):
                part = base
                for j in range(members):
                    if j != k:
                        one, other = r[0] ^ j, r[0] ^ k
                        ahead = one < other if forward else one > other
                        part = part + held[j] * ahead.astype(F32)
                outs[k][rows_of(h, shift if k == members - 1 else 0), :] = part.astype(BF16)
        for ref in gains:
            high = ref[...].astype(BF16)
            low = (ref[...] - high.astype(F32)).astype(BF16)
            for out in outs:
                rows = out.shape[0]
                out[rows - 2 * heads_all : rows - heads_all, :] = high
                out[rows - heads_all : rows, :] = low

    return layout.call(
        "spread", body, rank, [], [*got, *bases, *joined, *gain],
        [(layout.piece(extra), None)] * (members - 1) + [(layout.piece(extra + shift), None)], after=after,
        hint=hint,
    )


def scatter_back(layout, rank, got, bases, context, forward, mark, between, gain=None, hint=0):
    far, joined, pieces = layout.members - 1, [], []
    for c in range(layout.chunks):
        final = c == layout.chunks - 1
        mark = between(c, mark)
        rows = [gain()] if final and gain else []
        outs = spread(layout, rank, got[c], bases[c], forward, mark, joined if final else [], rows, hint)
        mark = [outs[0]]
        joined.append(outs[far])
        order = range(far if final else far - 1, 0, -1)
        moved = {k: swap(outs[k], "context", context, k) for k in order}
        pieces.append([(moved.get(k, outs[k]), 0) for k in range(layout.members)])
    if far:
        last = pieces[-1][far][0]
        for c, chunk in enumerate(pieces):
            chunk[far] = (last, c * layout.count * HD)
    return pieces, mark


def xor_steps(axis, size, stride):
    steps = []
    while stride < size:
        steps.append((axis, size, stride))
        stride *= 2
    return steps


def added(layout, rank, one, other, after):
    def body(r, one_ref, other_ref, out_ref):
        out_ref[...] = one_ref[...] + other_ref[...]

    return layout.call(
        "gain_sum", body, rank, [], [one, other], [(pltpu.VMEM(one.shape, F32), None)], after=after, moved=one.size * 12
    )[0]


def shards(dp, context, queries, keys, values, gain, out_grad):
    tokens, features = queries.shape[1:]
    members = divisor(context, (4, 2, 1))
    layout = Layout(tokens, features, members, CHUNKS)
    chunks = range(CHUNKS)
    place = (lax.axis_index("context") % members).astype(jnp.int32).reshape(1)
    q, k, v, g = (array[0] for array in (queries, keys, values, out_grad))
    gain_row = gain.reshape(1, features)

    k_kept, v_kept, got = [], [], []
    for c in chunks:
        k_c, v_c, states = block_states(layout, place, k, v, c)
        k_kept.append(k_c)
        v_kept.append(v_c)
        got.append(gather_home(states, context))
    inner, bases, mark = [], [], []
    for c in chunks:
        total = group_total(layout, place, got[c], mark)
        bases.append(cross_groups(total, members, context, True))
        inner.append(within_block(layout, place, q, g, gain_row, k_kept[c], v_kept[c], c, [total]))
        mark = [inner[c][3]]
    prior, mark = scatter_back(layout, place, got, bases, context, True, mark, lambda c, mark: mark)
    far = members - 1
    early = [(c, k) for c in chunks[:-1] for k in range(far)]
    middle = [(CHUNKS - 1, k) for k in range(far)]
    late = [(c, far) for c in chunks]
    mixed, sums = {}, []
    for group, hint in zip((early, middle, late), MIX_HINTS, strict=True):
        if group:
            mixed, sums = mix(layout, place, inner, prior, group, mixed, sums, hint)
    inv, factor = norm_factors(layout, place, *sums)

    d_mixed, got = [], []
    for c in chunks:
        q_c, g_c, gain_c = inner[c][:3]
        d_c, states = mixed_gradients(layout, place, mixed[c], q_c, g_c, gain_c, inv, factor)
        d_mixed.append(d_c)
        got.append(gather_home(states, context))

    normed, own, gain_grad = {}, [[] for _ in chunks], []
    regular = dp & (dp - 1) == 0 and context & (context - 1) == 0
    steps = xor_steps("dp", dp, 1) + xor_steps("context", context, members) if regular else []

    def inner_job(mark, c, part, hint=0, **beside):
        result = inner_gradients(
            layout, place, inner[c][4:], inner[c][0], k_kept[c], v_kept[c], d_mixed[c], prior[c], c, part, own[c], mark,
            hint=hint, **beside,
        )
        *own[c], token = result[:4]
        return [token], result[4:]

    def gain_job(mark):
        nonlocal gain_grad
        if not steps:
            return mark
        axis, size, stride = steps.pop(0)
        gain_grad = [added(layout, place, *gain_grad, swap(*gain_grad, axis, size, stride), mark)]
        return gain_grad

    cuts = sorted({0, members // 4, members // 2, members})
    jobs = [(0, part) for part in zip(cuts[:-1], cuts[1:], strict=True)]
    bases, mark = [], [d_mixed[-1]]
    for c in chunks:
        _, g_c, gain_c = inner[c][:3]
        normed[c], *gain_grad = normed_output(layout, place, mixed[c], g_c, gain_c, inv, c, gain_grad, mark)
        mark = gain_grad
        if c == CHUNKS - 1:
            mark, _ = inner_job(mark, *jobs.pop(0))
            mark = gain_job(mark)
        total = group_total(layout, place, got[c], mark)
        mark = [total]
        bases.append(cross_groups(total, members, context, False))


    def between(c, mark):
        if jobs:
            job = jobs.pop(0)
            mark, _ = inner_job(mark, *job)
        mark = gain_job(mark)
        while c == CHUNKS - 1 and steps:
            mark = gain_job(mark)
        return mark

    gain = (lambda: gain_grad[0]) if regular else None
    later, mark = scatter_back(layout, place, got, bases, context, False, mark, between, gain, SPREAD_HINT)
    also = [k_kept[0], v_kept[0], *own[0][1:], *[later[0][k][0] for k in range(far)]]
    others = [(c, own[c][0]) for c in chunks[:-1]]
    mark, (output, query_grad, *outer) = inner_job(
        mark, CHUNKS - 1, (0, members), OUTER_HINT, ready=[*normed.items()], others=others, also=also if far else []
    )
    *outer, query_grad, total_gain = [
        *outer_gradients(layout, place, k_kept, v_kept, own, later, middle + late, outer, regular, own[-1][0], query_grad), None
    ][:4]
    if not regular:
        total_gain = lax.psum(gain_grad[0], ("dp", "context"))
    return output[None], query_grad[None], outer[0][None], outer[1][None], total_gain.reshape(features)


def solution(mesh):
    sharded = P("dp", "context", None)
    return jax.shard_map(
        functools.partial(shards, mesh.shape["dp"], mesh.shape["context"]),
        mesh=mesh,
        in_specs=(sharded, sharded, sharded, P(), sharded),
        out_specs=(sharded, sharded, sharded, sharded, P()),
        check_vma=False,
    )
```

```python
import functools

import jax
import jax.numpy as jnp
from jax import lax
from jax.experimental import pallas as pl
from jax.experimental.pallas import tpu as pltpu
from jax.sharding import PartitionSpec as P

HD = 128
EPSILON = 1e-06
BF16 = jnp.bfloat16
F32 = jnp.float32
CHUNKS = 2
MIX_HINTS = (2, 1, 0)
OUTER_HINT = 2
SPREAD_HINT = 0
VMEM_LIMIT = 14 * 1024 * 1024


def dot(a, b, contract):
    return lax.dot_general(a, b, ((contract[:1], contract[1:]), ((), ())), preferred_element_type=F32)


def divisor(n, choices):
    return next(c for c in choices if n % c == 0)


def lanes(head):
    return slice(head * HD, (head + 1) * HD)


def resident(array):
    return pltpu.with_memory_space_constraint(array, pltpu.VMEM)


def pairs_of(count):
    step = 2 if count % 2 == 0 else 1
    return [range(h, h + step) for h in range(0, count, step)]


def rows_of(head, offset=0):
    return slice(offset + head * HD, offset + (head + 1) * HD)


def span(heads):
    return slice(heads[0] * HD, (heads[-1] + 1) * HD)


def diagonal(blocks):
    if len(blocks) == 1:
        return blocks[0]
    zero = jnp.zeros_like(blocks[0])
    return jnp.concatenate([jnp.concatenate([blocks[0], zero], 1), jnp.concatenate([zero, blocks[1]], 1)], 0)


HBM_WHOLE = pl.BlockSpec(memory_space=pl.ANY)


class Layout:
    def __init__(self, tokens, features, members, chunks):
        self.tokens = tokens
        self.features = features
        self.heads = features // HD
        self.members = members
        self.chunks = chunks
        self.count = self.heads // members // chunks
        self.width = self.count * HD
        self.size = self.count * members * tokens * HD

    def wide(self, chunk, first=0):
        chunks = self.chunks
        return pl.BlockSpec((self.tokens, self.width), lambda k, r: (0, (r[0] ^ (k + first)) * chunks + chunk))

    def columns(self, r, piece, chunk):
        return pl.ds(pl.multiple_of(((r[0] ^ piece) * self.chunks + chunk) * self.width, self.width), self.width)

    def wide_shape(self, kind=BF16):
        return jax.ShapeDtypeStruct((self.tokens, self.features), kind)

    def row_shape(self):
        return jax.ShapeDtypeStruct((1, self.features), F32)

    def kept(self, kind):
        return pltpu.VMEM((self.members, self.tokens, self.width), kind)

    def kept_row(self):
        return pltpu.VMEM((self.members, 1, self.width), F32)

    def narrow(self):
        return pltpu.VMEM((self.tokens, HD), F32)

    def piece(self, extra=0):
        return pltpu.VMEM((self.count * HD + extra, HD), BF16)

    def cut(self):
        return self.tokens // 256 * 256 if self.tokens > 256 and self.tokens % 256 % 16 == 0 else self.tokens

    def weights(self):
        cut, rest = self.cut(), max(self.tokens - self.cut(), 16)
        lead = (self.members, self.count)
        return [pltpu.VMEM((*lead, self.tokens, cut), BF16), pltpu.VMEM((*lead, rest, rest), BF16)]

    def token(self):
        return pltpu.VMEM((8, HD), F32)

    def call(self, name, body, rank, streamed, held, outs, after=(), into=(), macs=0, moved=0, scratch=(), grid=(1,), hint=0):
        whole = pl.BlockSpec(memory_space=pltpu.VMEM)
        unread = pl.BlockSpec(memory_space=pl.ANY)
        operands = [pltpu.with_memory_space_constraint(a, pltpu.HBM) for a in streamed]
        operands += [resident(a) for a in [*held, *after]]
        operands += [pltpu.with_memory_space_constraint(a, memory) for a, _, memory in into]
        first = 1 + len(streamed) + len(held) + len(after)
        used = len(streamed) + len(held)
        skipped = len(after) + len(into)

        def kernel(r, *refs):
            body(r, *refs[:used], *refs[used + skipped :])

        return pl.pallas_call(
            kernel,
            name=name,
            grid_spec=pltpu.PrefetchScalarGridSpec(
                num_scalar_prefetch=1,
                grid=grid,
                in_specs=[unread] * len(streamed) + [whole] * len(held) + [unread] * skipped,
                out_specs=[whole if s is None else s for _, s in outs],
                scratch_shapes=list(scratch),
            ),
            out_shape=[s for s, _ in outs],
            input_output_aliases={first + n: at for n, (_, at, _) in enumerate(into)},
            compiler_params=pltpu.CompilerParams(vmem_limit_bytes=VMEM_LIMIT),
            cost_estimate=pl.CostEstimate(
                flops=int(hint * 1e9) + 1, bytes_accessed=int(hint * 3.6e6) + 1, transcendentals=0
            ),
        )(rank, *operands)


def for_piece(refs, act):
    for k, ref in enumerate(refs):

        @pl.when(pl.program_id(0) == k)
        def _(ref=ref):
            act(ref)


def block_states(layout, rank, keys, values, chunk):
    members = layout.members

    def body(r, k_hbm, v_hbm, k_out, v_out, *refs):
        outs, sems = refs[:members], refs[members]
        copies = []
        for piece in range(members):
            at = layout.columns(r, piece, chunk)
            copies.append(pltpu.make_async_copy(k_hbm.at[:, at], k_out.at[piece], sems.at[0, piece]))
            copies.append(pltpu.make_async_copy(v_hbm.at[:, at], v_out.at[piece], sems.at[1, piece]))
        for copy in copies:
            copy.start()
        for piece in range(members):
            copies[2 * piece].wait()
            copies[2 * piece + 1].wait()
            states = [dot(k_out[piece, :, lanes(h)], v_out[piece, :, lanes(h)], (0, 0)) for h in range(layout.count)]
            for h, state in enumerate(states):
                outs[piece][lanes(h), :] = state.astype(BF16)

    k, v, *states = layout.call(
        "block_states", body, rank, [keys, values], [],
        [(layout.kept(BF16), None)] * 2 + [(layout.piece(), None)] * members,
        macs=layout.size * HD, moved=4 * layout.size, scratch=[pltpu.SemaphoreType.DMA((2, members))],
    )
    return k, v, states


def masked(product):
    rows = lax.broadcasted_iota(jnp.int32, product.shape, 0)
    columns = lax.broadcasted_iota(jnp.int32, product.shape, 1)
    return jnp.where(rows >= columns, product, 0.0).astype(BF16)


def masked_product(a, b, cut):
    blocks = [masked(dot(a, b[:cut], (1, 1)))]
    if cut < a.shape[0]:
        blocks.append(masked(dot(a[cut:], b[cut:], (1, 1))))
    return blocks


def store_product(out, at, blocks, b, cut, add=None):
    rows, columns = at[1:] if len(at) == 3 else at
    lead = at[:-2]
    full = dot(blocks[0], b[:cut], (1, 0))
    full = full if add is None else full + add
    out[(*lead, slice(0, cut), columns)] = full[:cut].astype(out.dtype)
    if len(blocks) > 1:
        out[(*lead, slice(cut, None), columns)] = (full[cut:] + dot(blocks[1], b[cut:], (1, 0))).astype(out.dtype)


def store_turned(out, at, blocks, b, cut):
    lead, columns = at[:-2], at[-1]
    out[(*lead, slice(0, cut), columns)] = dot(blocks[0], b, (0, 0))
    if len(blocks) > 1:
        out[(*lead, slice(cut, None), columns)] = dot(blocks[1], b[cut:], (0, 0))


def within_block(layout, rank, queries, out_grad, gain, keys, values, chunk, after):
    members = layout.members

    def body(r, q_hbm, g_hbm, gain_ref, k_ref, v_ref, q_out, g_out, gain_out, o_ref, *refs):
        w_refs, sems = refs[:-1], refs[-1]
        q_copies, g_copies = [], []
        for piece in range(members):
            at = layout.columns(r, piece, chunk)
            q_copies.append(pltpu.make_async_copy(q_hbm.at[:, at], q_out.at[piece], sems.at[0, piece]))
            g_copies.append(pltpu.make_async_copy(g_hbm.at[:, at], g_out.at[piece], sems.at[1, piece]))
        for copy in q_copies + g_copies:
            copy.start()
        for piece in range(members):
            gain_out[piece] = gain_ref[:, layout.columns(r, piece, chunk)]
            q_copies[piece].wait()
            weights = []
            for h in range(layout.count):
                weights.append(masked_product(q_out[piece, :, lanes(h)], k_ref[piece, :, lanes(h)], layout.cut()))
            for h in range(layout.count):
                for w_ref, block in zip(w_refs, weights[h]):
                    w_ref[piece, h] = block
                store_product(o_ref, (piece, slice(None), lanes(h)), weights[h], v_ref[piece, :, lanes(h)], layout.cut())
        for copy in g_copies:
            copy.wait()

    return layout.call(
        "within_block", body, rank, [queries, out_grad], [gain, keys, values],
        [(layout.kept(BF16), None)] * 2 + [(layout.kept_row(), None), (layout.kept(F32), None)]
        + [(shape, None) for shape in layout.weights()],
        after=after, macs=2 * layout.size * layout.tokens, moved=4 * layout.size, scratch=[pltpu.SemaphoreType.DMA((2, members))],
    )


def mix(layout, rank, kept, prior, jobs, mixed, sums, final, hint):
    chunks = sorted({c for c, _ in jobs})
    fields = [kept[c][n] for c in chunks for n in (3, 0, 1, 2)]
    states = [prior[c][k][0] for c, k in jobs]
    old = [(n, mixed[c]) for n, c in enumerate(chunks) if c in mixed]

    def body(r, *refs):
        fields_in, refs = refs[: len(fields)], refs[len(fields) :]
        state_refs, refs = refs[: len(jobs)], refs[len(jobs) :]
        before, (*m_refs, square_ref, cross_ref) = refs[: len(sums)], refs[len(sums) :]
        square = before[0][...] if sums else jnp.zeros(square_ref.shape, F32)
        cross = before[1][...] if sums else jnp.zeros(cross_ref.shape, F32)
        for (c, piece), state in zip(jobs, state_refs, strict=True):
            n, offset = chunks.index(c), prior[c][piece][1]
            o_ref, q_ref, g_ref, gain_ref = fields_in[4 * n : 4 * n + 4]
            products = []
            for heads in pairs_of(layout.count):
                block = diagonal([state[rows_of(h, offset), :] for h in heads])
                both = dot(q_ref[piece, :, span(heads)], block, (1, 0))
                products += [both[:, lanes(m)] for m in range(len(heads))]
            for h in range(layout.count):
                at = (piece, slice(None), lanes(h))
                value = o_ref[at] + products[h]
                m_refs[n][at] = value
                square = square + value * value
                cross = cross + gain_ref[piece, :, lanes(h)] * g_ref[at].astype(F32) * value
        if final:
            inv = lax.rsqrt(jnp.sum(square, -1, keepdims=True) / layout.features + EPSILON)
            centered = jnp.sum(cross, -1, keepdims=True) / layout.features
            square = jnp.broadcast_to(inv, square.shape)
            cross = jnp.broadcast_to(inv * inv * inv * centered, cross.shape)
        square_ref[...] = square
        cross_ref[...] = cross

    *outs, square, cross = layout.call(
        "mix", body, rank, [], [*fields, *states, *sums],
        [(layout.kept(F32), None)] * len(chunks) + [(layout.narrow(), None)] * 2,
        into=[(a, n, pltpu.VMEM) for n, a in old], hint=hint,
    )
    return {**mixed, **dict(zip(chunks, outs, strict=True))}, [square, cross]


def mixed_gradients(layout, rank, mixed, queries, out_grad, gain, inv, factor):
    def body(r, m_ref, q_ref, g_ref, gain_ref, inv_ref, factor_ref, d_ref, *outs):
        piece = pl.program_id(0)

        def act(out):
            for h in range(layout.count):
                at = (piece, slice(None), lanes(h))
                scaled = gain_ref[piece, :, lanes(h)] * g_ref[at].astype(F32)
                grad = (inv_ref[...] * scaled - m_ref[at] * factor_ref[...]).astype(BF16)
                d_ref[at] = grad
                out[lanes(h), :] = dot(q_ref[at], grad, (0, 0)).astype(BF16)

        for_piece(outs, act)

    d_mixed, *states = layout.call(
        "mixed_gradients", body, rank, [], [mixed, queries, out_grad, gain, inv, factor],
        [(layout.kept(BF16), None)] + [(layout.piece(), None)] * layout.members,
        macs=layout.size * HD, moved=layout.size, grid=(layout.members,),
    )
    return d_mixed, states


def normed_output(layout, rank, mixed, out_grad, gain, inv, chunk, gain_grad, after):
    def body(r, m_ref, g_ref, gain_ref, inv_ref, o_ref, part_ref):
        for piece in range(layout.members):
            for h in range(layout.count):
                here = (piece, slice(None), lanes(h))
                normed = m_ref[here] * inv_ref[...]
                o_ref[here] = (normed * gain_ref[piece, :, lanes(h)]).astype(BF16)
                head = ((r[0] ^ piece) * layout.chunks + chunk) * layout.count + h
                part_ref[pl.ds(head, 1), :] = jnp.sum(g_ref[here].astype(F32) * normed, 0, keepdims=True)

    return layout.call(
        "normed_output", body, rank, [], [mixed, out_grad, gain, inv],
        [(layout.kept(BF16), None), (pltpu.VMEM((layout.heads, HD), F32), None)],
        into=[(a, 1, pltpu.VMEM) for a in gain_grad], after=after,
    )


def inner_gradients(
    layout, rank, weights, queries, keys, values, d_mixed, prior, chunk, part, own, after, ready=(), others=(), also=(), hint=0
):
    first, last = part
    targets = ([0] if ready else []) + ([1] if others else []) + ([2, 3] if also else [])
    hbm = [(layout.wide_shape(), HBM_WHOLE)] * len(targets)
    lists = [*((0, c, a) for c, a in ready), *((1, c, a) for c, a in others)]
    extra = max(len(also) - 4, 0)

    def body(r, *refs):
        w_refs, (q_ref, k_ref, v_ref, d_ref, *refs) = refs[: len(weights)], refs[len(weights) :]
        states, refs = refs[: last - first], refs[last - first :]
        list_refs, refs = refs[: len(lists)], refs[len(lists) :]
        also_refs, (dq_ref, dk_ref, dv_ref, token_ref, *refs) = refs[: len(also)], refs[len(also) :]
        hbm_refs, (state, dk_buffer, dv_buffer, sems) = dict(zip(targets, refs)), refs[len(hbm) :]
        step = pl.program_id(0)
        piece = step + first
        token_ref[...] = jnp.zeros_like(token_ref)

        def write(n, c, source, at):
            target = hbm_refs[n].at[:, layout.columns(r, at, c)]
            return pltpu.make_async_copy(source.at[at], target, sems.at[n * layout.chunks + c, at])

        def list_copies():
            for (n, c, _), ref in zip(lists, list_refs, strict=True):
                for at in range(layout.members):
                    yield write(n, c, ref, at)

        def outer_copies(at):
            return [write(n, 0, ref, at) for n, ref in ((2, dk_buffer), (3, dv_buffer))]

        @pl.when(step == 0)
        def _():
            for copy in list_copies():
                copy.start()

        for n, (ref, (_, offset)) in enumerate(zip(states, prior[first:last], strict=True)):

            @pl.when(step == n)
            def _(ref=ref, offset=offset):
                state[...] = ref[offset : offset + layout.count * HD, :]

        for n in range(extra):

            @pl.when(step == n)
            def _(n=n):
                store_outer(layout, also_refs[:4], also_refs[4 + n], 0, n, dk_buffer, dv_buffer, n)
                for copy in outer_copies(n):
                    copy.start()

        d_weights, from_prior = [], []
        for h in range(layout.count):
            at = (piece, slice(None), lanes(h))
            d_weights.append(masked_product(d_ref[at], v_ref[at], layout.cut()))
        for heads in pairs_of(layout.count):
            both = dot(d_ref[piece, :, span(heads)], diagonal([state[lanes(h), :] for h in heads]), (1, 1))
            from_prior += [both[:, lanes(n)] for n in range(len(heads))]
        for h in range(layout.count):
            at = (piece, slice(None), lanes(h))
            kept = [w_ref[piece, h] for w_ref in w_refs][: len(d_weights[h])]
            store_product(dq_ref, at, d_weights[h], k_ref[at], layout.cut(), from_prior[h])
            store_turned(dk_ref, at, d_weights[h], q_ref[at], layout.cut())
            store_turned(dv_ref, at, kept, d_ref[at], layout.cut())
        if others:

            @pl.when(step < last - first - 1)
            def _():
                write(1, chunk, dq_ref, piece).start()

        @pl.when(step == last - first - 1)
        def _():
            for copy in list_copies():
                copy.wait()
            for at in range(first, last - 1 if others else first):
                write(1, chunk, dq_ref, at).wait()
            for n in range(extra):
                for copy in outer_copies(n):
                    copy.wait()

    buffer = pltpu.VMEM((max(extra, 1), layout.tokens, layout.width), BF16)
    return layout.call(
        "inner_gradients", body, rank, [],
        [*weights, queries, keys, values, d_mixed, *[a for a, _ in prior[first:last]], *[a for _, _, a in lists], *also],
        [(layout.kept(BF16), None), (layout.kept(F32), None), (layout.kept(F32), None), (layout.token(), None)] + hbm,
        into=[(a, n, pltpu.VMEM) for n, a in enumerate(own)], after=after, hint=hint,
        scratch=[
            pltpu.VMEM((layout.count * HD, HD), BF16), buffer, buffer,
            pltpu.SemaphoreType.DMA((4 * layout.chunks, layout.members)),
        ],
        grid=(last - first,),
    )


def store_outer(layout, fields, state, offset, piece, dk_buffer, dv_buffer, slot):
    k_ref, v_ref, dki_ref, dvi_ref = fields
    sums = []
    for heads in pairs_of(layout.count):
        here = (piece, slice(None), span(heads))
        block = diagonal([state[rows_of(h, offset), :] for h in heads])
        sums.append((heads, here, dot(v_ref[here], block, (1, 1)), dot(k_ref[here], block, (1, 0))))
    for heads, here, dk, dv in sums:
        dk_buffer[slot, :, span(heads)] = (dki_ref[here] + dk).astype(BF16)
        dv_buffer[slot, :, span(heads)] = (dvi_ref[here] + dv).astype(BF16)


def pairwise(terms):
    while len(terms) > 1:
        terms = [a + b for a, b in zip(terms[::2], terms[1::2], strict=True)]
    return terms[0]


def outer_gradients(layout, rank, keys, values, own, later, jobs, into, extra, queries, query_grad):
    chunks = sorted({c for c, _ in jobs})
    fields = [a for c in chunks for a in (keys[c], values[c], *own[c][1:])]
    states = [later[c][k][0] for c, k in jobs]
    count, heads_all = len(jobs), layout.heads
    gain_out = [(jax.ShapeDtypeStruct((heads_all, HD), F32), HBM_WHOLE)] if extra else []

    def body(r, *refs):
        fields_in, refs = refs[: len(fields)], refs[len(fields) :]
        state_refs, (q_ref, dk_hbm, dv_hbm, dq_hbm, *refs) = refs[:count], refs[count:]
        gain_hbm, (dk_buffer, dv_buffer, gain_buffer, sems) = refs[: len(gain_out)], refs[len(gain_out) :]
        at = layout.columns(r, layout.members - 1, layout.chunks - 1)
        copies = [pltpu.make_async_copy(q_ref.at[layout.members - 1], dq_hbm.at[:, at], sems.at[3, 0])]
        copies[0].start()
        if extra:
            parts = []
            for _, n in sorted((piece, n) for n, (c, piece) in enumerate(jobs) if c == chunks[-1]):
                rows = state_refs[n][-2 * heads_all :, :].astype(F32)
                parts.append(rows[:heads_all] + rows[heads_all:])
            gain_buffer[...] = pairwise(parts)
            copies.append(pltpu.make_async_copy(gain_buffer, gain_hbm[0], sems.at[2, 0]))
            copies[-1].start()
        for n, ((c, piece), state) in enumerate(zip(jobs, state_refs, strict=True)):
            at, offset = layout.columns(r, piece, c), later[c][piece][1]
            here = 4 * chunks.index(c)
            store_outer(layout, fields_in[here : here + 4], state, offset, piece, dk_buffer, dv_buffer, n)
            copies.append(pltpu.make_async_copy(dk_buffer.at[n], dk_hbm.at[:, at], sems.at[0, n]))
            copies.append(pltpu.make_async_copy(dv_buffer.at[n], dv_hbm.at[:, at], sems.at[1, n]))
            copies[-2].start()
            copies[-1].start()
        for copy in copies:
            copy.wait()

    return layout.call(
        "outer_gradients", body, rank, [], [*fields, *states, queries],
        [(layout.wide_shape(), HBM_WHOLE)] * 3 + gain_out,
        into=[(a, n, pltpu.HBM) for n, a in enumerate(into)] + [(query_grad, 2, pltpu.HBM)],
        scratch=[pltpu.VMEM((count, layout.tokens, layout.width), BF16)] * 2
        + [pltpu.VMEM((heads_all, HD), F32), pltpu.SemaphoreType.DMA((4, count))],
    )


def swap(array, axis, size, k):
    return lax.ppermute(array, axis, [(c, c ^ k) for c in range(size)])


def gather_home(pieces, context):
    order = range(len(pieces) - 1, 0, -1)
    got = {k: swap(pieces[k], "context", context, k) for k in order}
    return [pieces[0]] + [got[k] for k in range(1, len(pieces))]


def group_total(layout, rank, got, after):
    def body(r, *refs):
        *gots, total = refs
        total[...] = sum(g[...].astype(F32) for g in gots).astype(BF16)

    return layout.call(
        "group_total", body, rank, [], got, [(layout.piece(), None)], after=after, moved=layout.count * HD * HD * 10
    )[0]


def cross_groups(total, members, context, forward):
    bases = []
    for far in range(1, context // members):
        hop = far * members
        up = [(c, c + hop) for c in range(context - hop)]
        bases.append(lax.ppermute(total, "context", up if forward else [(b, a) for a, b in up]))
    return bases


def spread(layout, rank, got, bases, forward, after, joined=(), gain=(), hint=0):
    members, heads_all = layout.members, layout.heads
    extra = 2 * heads_all * len(gain)
    shift = layout.count * HD * len(joined)

    def body(r, *refs):
        gots, rest = refs[:members], refs[members:]
        lows, rest = rest[: len(bases)], rest[len(bases) :]
        joined_refs, rest = rest[: len(joined)], rest[len(joined) :]
        gains, outs = rest[: len(gain)], rest[len(gain) :]
        for n, ref in enumerate(joined_refs):
            outs[-1][n * layout.count * HD : (n + 1) * layout.count * HD, :] = ref[...]
        for h in range(layout.count):
            held = [g[rows_of(h), :].astype(F32) for g in gots]
            base = sum((low[rows_of(h), :].astype(F32) for low in lows), jnp.zeros((HD, HD), F32))
            for k in range(members):
                part = base
                for j in range(members):
                    if j != k:
                        one, other = r[0] ^ j, r[0] ^ k
                        ahead = one < other if forward else one > other
                        part = part + held[j] * ahead.astype(F32)
                outs[k][rows_of(h, shift if k == members - 1 else 0), :] = part.astype(BF16)
        for ref in gains:
            high = ref[...].astype(BF16)
            low = (ref[...] - high.astype(F32)).astype(BF16)
            for out in outs:
                rows = out.shape[0]
                out[rows - 2 * heads_all : rows - heads_all, :] = high
                out[rows - heads_all : rows, :] = low

    return layout.call(
        "spread", body, rank, [], [*got, *bases, *joined, *gain],
        [(layout.piece(extra), None)] * (members - 1) + [(layout.piece(extra + shift), None)], after=after,
        hint=hint,
    )


def scatter_back(layout, rank, got, bases, context, forward, mark, between, gain=None, hint=0):
    far, joined, pieces = layout.members - 1, [], []
    for c in range(layout.chunks):
        final = c == layout.chunks - 1
        mark = between(c, mark)
        rows = [gain()] if final and gain else []
        outs = spread(layout, rank, got[c], bases[c], forward, mark, joined if final else [], rows, hint)
        mark = [outs[0]]
        joined.append(outs[far])
        order = range(far if final else far - 1, 0, -1)
        moved = {k: swap(outs[k], "context", context, k) for k in order}
        pieces.append([(moved.get(k, outs[k]), 0) for k in range(layout.members)])
    if far:
        last = pieces[-1][far][0]
        for c, chunk in enumerate(pieces):
            chunk[far] = (last, c * layout.count * HD)
    return pieces, mark


def xor_steps(axis, size, stride):
    steps = []
    while stride < size:
        steps.append((axis, size, stride))
        stride *= 2
    return steps


def added(layout, rank, one, other, after):
    def body(r, one_ref, other_ref, out_ref):
        out_ref[...] = one_ref[...] + other_ref[...]

    return layout.call(
        "gain_sum", body, rank, [], [one, other], [(pltpu.VMEM(one.shape, F32), None)], after=after, moved=one.size * 12
    )[0]


def shards(dp, context, queries, keys, values, gain, out_grad):
    tokens, features = queries.shape[1:]
    members = divisor(context, (4, 2, 1))
    layout = Layout(tokens, features, members, CHUNKS)
    chunks = range(CHUNKS)
    place = (lax.axis_index("context") % members).astype(jnp.int32).reshape(1)
    q, k, v, g = (array[0] for array in (queries, keys, values, out_grad))
    gain_row = gain.reshape(1, features)

    k_kept, v_kept, got = [], [], []
    for c in chunks:
        k_c, v_c, states = block_states(layout, place, k, v, c)
        k_kept.append(k_c)
        v_kept.append(v_c)
        got.append(gather_home(states, context))
    inner, bases, mark = [], [], []
    for c in chunks:
        total = group_total(layout, place, got[c], mark)
        bases.append(cross_groups(total, members, context, True))
        inner.append(within_block(layout, place, q, g, gain_row, k_kept[c], v_kept[c], c, [total]))
        mark = [inner[c][3]]
    prior, mark = scatter_back(layout, place, got, bases, context, True, mark, lambda c, mark: mark)
    far = members - 1
    early = [(c, k) for c in chunks[:-1] for k in range(far)]
    middle = [(CHUNKS - 1, k) for k in range(far)] or [(c, 0) for c in chunks]
    late = [(c, far) for c in chunks] if far else []
    mixed, sums = {}, []
    for group, hint in zip((early, late, middle), MIX_HINTS, strict=True):
        if group:
            mixed, sums = mix(layout, place, inner, prior, group, mixed, sums, group == middle, hint)
    inv, factor = sums

    d_mixed, got = [], []
    for c in chunks:
        q_c, g_c, gain_c = inner[c][:3]
        d_c, states = mixed_gradients(layout, place, mixed[c], q_c, g_c, gain_c, inv, factor)
        d_mixed.append(d_c)
        got.append(gather_home(states, context))

    normed, own, gain_grad = {}, [[] for _ in chunks], []
    regular = dp & (dp - 1) == 0 and context & (context - 1) == 0
    steps = xor_steps("dp", dp, 1) + xor_steps("context", context, members) if regular else []

    def inner_job(mark, c, part, hint=0, **beside):
        result = inner_gradients(
            layout, place, inner[c][4:], inner[c][0], k_kept[c], v_kept[c], d_mixed[c], prior[c], c, part, own[c], mark,
            hint=hint, **beside,
        )
        *own[c], token = result[:4]
        return [token], result[4:]

    def gain_job(mark):
        nonlocal gain_grad
        if not steps:
            return mark
        axis, size, stride = steps.pop(0)
        gain_grad = [added(layout, place, *gain_grad, swap(*gain_grad, axis, size, stride), mark)]
        return gain_grad

    cuts = sorted({0, members // 4, members // 2, members})
    jobs = [(0, part) for part in zip(cuts[:-1], cuts[1:], strict=True)]
    bases, mark = [], [d_mixed[-1]]
    for c in chunks:
        _, g_c, gain_c = inner[c][:3]
        normed[c], *gain_grad = normed_output(layout, place, mixed[c], g_c, gain_c, inv, c, gain_grad, mark)
        mark = gain_grad
        if c == CHUNKS - 1:
            mark, _ = inner_job(mark, *jobs.pop(0))
            mark = gain_job(mark)
        total = group_total(layout, place, got[c], mark)
        mark = [total]
        bases.append(cross_groups(total, members, context, False))


    def between(c, mark):
        if jobs:
            job = jobs.pop(0)
            mark, _ = inner_job(mark, *job)
        mark = gain_job(mark)
        while c == CHUNKS - 1 and steps:
            mark = gain_job(mark)
        return mark

    gain = (lambda: gain_grad[0]) if regular else None
    later, mark = scatter_back(layout, place, got, bases, context, False, mark, between, gain, SPREAD_HINT)
    also = [k_kept[0], v_kept[0], *own[0][1:], *[later[0][k][0] for k in range(far)]]
    others = [(c, own[c][0]) for c in chunks[:-1]]
    mark, (output, query_grad, *outer) = inner_job(
        mark, CHUNKS - 1, (0, members), OUTER_HINT, ready=[*normed.items()], others=others, also=also if far else []
    )
    *outer, query_grad, total_gain = [
        *outer_gradients(layout, place, k_kept, v_kept, own, later, middle + late, outer, regular, own[-1][0], query_grad), None
    ][:4]
    if not regular:
        total_gain = lax.psum(gain_grad[0], ("dp", "context"))
    return output[None], query_grad[None], outer[0][None], outer[1][None], total_gain.reshape(features)


def solution(mesh):
    sharded = P("dp", "context", None)
    return jax.shard_map(
        functools.partial(shards, mesh.shape["dp"], mesh.shape["context"]),
        mesh=mesh,
        in_specs=(sharded, sharded, sharded, P(), sharded),
        out_specs=(sharded, sharded, sharded, sharded, P()),
        check_vma=False,
    )
```

```python
import functools

import jax
import jax.numpy as jnp
from jax import lax
from jax.experimental import pallas as pl
from jax.experimental.pallas import tpu as pltpu
from jax.sharding import PartitionSpec as P

HD = 128
EPSILON = 1e-06
BF16 = jnp.bfloat16
F32 = jnp.float32
CHUNKS = 2
MIX_HINTS = (2, 1, 0)
OUTER_HINT = 2
SPREAD_HINT = 0
VMEM_LIMIT = 14 * 1024 * 1024


def dot(a, b, contract):
    return lax.dot_general(a, b, ((contract[:1], contract[1:]), ((), ())), preferred_element_type=F32)


def divisor(n, choices):
    return next(c for c in choices if n % c == 0)


def lanes(head):
    return slice(head * HD, (head + 1) * HD)


def resident(array):
    return pltpu.with_memory_space_constraint(array, pltpu.VMEM)


def pairs_of(count):
    step = 2 if count % 2 == 0 else 1
    return [range(h, h + step) for h in range(0, count, step)]


def rows_of(head, offset=0):
    return slice(offset + head * HD, offset + (head + 1) * HD)


def span(heads):
    return slice(heads[0] * HD, (heads[-1] + 1) * HD)


def diagonal(blocks):
    if len(blocks) == 1:
        return blocks[0]
    zero = jnp.zeros_like(blocks[0])
    return jnp.concatenate([jnp.concatenate([blocks[0], zero], 1), jnp.concatenate([zero, blocks[1]], 1)], 0)


HBM_WHOLE = pl.BlockSpec(memory_space=pl.ANY)


class Layout:
    def __init__(self, tokens, features, members, chunks):
        self.tokens = tokens
        self.features = features
        self.heads = features // HD
        self.members = members
        self.chunks = chunks
        self.count = self.heads // members // chunks
        self.width = self.count * HD
        self.size = self.count * members * tokens * HD

    def wide(self, chunk, first=0):
        chunks = self.chunks
        return pl.BlockSpec((self.tokens, self.width), lambda k, r: (0, (r[0] ^ (k + first)) * chunks + chunk))

    def columns(self, r, piece, chunk):
        return pl.ds(pl.multiple_of(((r[0] ^ piece) * self.chunks + chunk) * self.width, self.width), self.width)

    def wide_shape(self, kind=BF16):
        return jax.ShapeDtypeStruct((self.tokens, self.features), kind)

    def row_shape(self):
        return jax.ShapeDtypeStruct((1, self.features), F32)

    def kept(self, kind):
        return pltpu.VMEM((self.members, self.tokens, self.width), kind)

    def kept_row(self):
        return pltpu.VMEM((self.members, 1, self.width), F32)

    def narrow(self):
        return pltpu.VMEM((self.tokens, HD), F32)

    def piece(self, extra=0):
        return pltpu.VMEM((self.count * HD + extra, HD), BF16)

    def cut(self):
        return self.tokens // 256 * 256 if self.tokens > 256 and self.tokens % 256 % 16 == 0 else self.tokens

    def weights(self):
        cut, rest = self.cut(), max(self.tokens - self.cut(), 16)
        lead = (self.members, self.count)
        return [pltpu.VMEM((*lead, self.tokens, cut), BF16), pltpu.VMEM((*lead, rest, rest), BF16)]

    def token(self):
        return pltpu.VMEM((8, HD), F32)

    def call(self, name, body, rank, streamed, held, outs, after=(), into=(), macs=0, moved=0, scratch=(), grid=(1,), hint=0):
        whole = pl.BlockSpec(memory_space=pltpu.VMEM)
        unread = pl.BlockSpec(memory_space=pl.ANY)
        operands = [pltpu.with_memory_space_constraint(a, pltpu.HBM) for a in streamed]
        operands += [resident(a) for a in [*held, *after]]
        operands += [pltpu.with_memory_space_constraint(a, memory) for a, _, memory in into]
        first = 1 + len(streamed) + len(held) + len(after)
        used = len(streamed) + len(held)
        skipped = len(after) + len(into)

        def kernel(r, *refs):
            body(r, *refs[:used], *refs[used + skipped :])

        return pl.pallas_call(
            kernel,
            name=name,
            grid_spec=pltpu.PrefetchScalarGridSpec(
                num_scalar_prefetch=1,
                grid=grid,
                in_specs=[unread] * len(streamed) + [whole] * len(held) + [unread] * skipped,
                out_specs=[whole if s is None else s for _, s in outs],
                scratch_shapes=list(scratch),
            ),
            out_shape=[s for s, _ in outs],
            input_output_aliases={first + n: at for n, (_, at, _) in enumerate(into)},
            compiler_params=pltpu.CompilerParams(vmem_limit_bytes=VMEM_LIMIT),
            cost_estimate=pl.CostEstimate(
                flops=int(hint * 1e9) + 1, bytes_accessed=int(hint * 3.6e6) + 1, transcendentals=0
            ),
        )(rank, *operands)


def for_piece(refs, act):
    for k, ref in enumerate(refs):

        @pl.when(pl.program_id(0) == k)
        def _(ref=ref):
            act(ref)


def block_states(layout, rank, keys, values, chunk):
    members = layout.members

    def body(r, k_hbm, v_hbm, k_out, v_out, *refs):
        outs, sems = refs[:members], refs[members]
        copies = []
        for piece in range(members):
            at = layout.columns(r, piece, chunk)
            copies.append(pltpu.make_async_copy(k_hbm.at[:, at], k_out.at[piece], sems.at[0, piece]))
            copies.append(pltpu.make_async_copy(v_hbm.at[:, at], v_out.at[piece], sems.at[1, piece]))
        for copy in copies:
            copy.start()
        for piece in range(members):
            copies[2 * piece].wait()
            copies[2 * piece + 1].wait()
            states = [dot(k_out[piece, :, lanes(h)], v_out[piece, :, lanes(h)], (0, 0)) for h in range(layout.count)]
            for h, state in enumerate(states):
                outs[piece][lanes(h), :] = state.astype(BF16)

    k, v, *states = layout.call(
        "block_states", body, rank, [keys, values], [],
        [(layout.kept(BF16), None)] * 2 + [(layout.piece(), None)] * members,
        macs=layout.size * HD, moved=4 * layout.size, scratch=[pltpu.SemaphoreType.DMA((2, members))],
    )
    return k, v, states


def masked(product):
    rows = lax.broadcasted_iota(jnp.int32, product.shape, 0)
    columns = lax.broadcasted_iota(jnp.int32, product.shape, 1)
    return jnp.where(rows >= columns, product, 0.0).astype(BF16)


def masked_product(a, b, cut):
    blocks = [masked(dot(a, b[:cut], (1, 1)))]
    if cut < a.shape[0]:
        blocks.append(masked(dot(a[cut:], b[cut:], (1, 1))))
    return blocks


def store_product(out, at, blocks, b, cut, add=None):
    rows, columns = at[1:] if len(at) == 3 else at
    lead = at[:-2]
    full = dot(blocks[0], b[:cut], (1, 0))
    full = full if add is None else full + add
    out[(*lead, slice(0, cut), columns)] = full[:cut].astype(out.dtype)
    if len(blocks) > 1:
        out[(*lead, slice(cut, None), columns)] = (full[cut:] + dot(blocks[1], b[cut:], (1, 0))).astype(out.dtype)


def store_turned(out, at, blocks, b, cut):
    lead, columns = at[:-2], at[-1]
    out[(*lead, slice(0, cut), columns)] = dot(blocks[0], b, (0, 0))
    if len(blocks) > 1:
        out[(*lead, slice(cut, None), columns)] = dot(blocks[1], b[cut:], (0, 0))


def within_block(layout, rank, queries, out_grad, gain, keys, values, chunk, after):
    members = layout.members

    def body(r, q_hbm, g_hbm, gain_ref, k_ref, v_ref, q_out, g_out, gain_out, o_ref, *refs):
        w_refs, sems = refs[:-1], refs[-1]
        q_copies, g_copies = [], []
        for piece in range(members):
            at = layout.columns(r, piece, chunk)
            q_copies.append(pltpu.make_async_copy(q_hbm.at[:, at], q_out.at[piece], sems.at[0, piece]))
            g_copies.append(pltpu.make_async_copy(g_hbm.at[:, at], g_out.at[piece], sems.at[1, piece]))
        for copy in q_copies + g_copies:
            copy.start()
        for piece in range(members):
            gain_out[piece] = gain_ref[:, layout.columns(r, piece, chunk)]
            q_copies[piece].wait()
            weights = []
            for h in range(layout.count):
                weights.append(masked_product(q_out[piece, :, lanes(h)], k_ref[piece, :, lanes(h)], layout.cut()))
            for h in range(layout.count):
                for w_ref, block in zip(w_refs, weights[h]):
                    w_ref[piece, h] = block
                store_product(o_ref, (piece, slice(None), lanes(h)), weights[h], v_ref[piece, :, lanes(h)], layout.cut())
        for copy in g_copies:
            copy.wait()

    return layout.call(
        "within_block", body, rank, [queries, out_grad], [gain, keys, values],
        [(layout.kept(BF16), None)] * 2 + [(layout.kept_row(), None), (layout.kept(F32), None)]
        + [(shape, None) for shape in layout.weights()],
        after=after, macs=2 * layout.size * layout.tokens, moved=4 * layout.size, scratch=[pltpu.SemaphoreType.DMA((2, members))],
    )


def mix(layout, rank, kept, prior, jobs, mixed, sums, final, hint):
    chunks = sorted({c for c, _ in jobs})
    fields = [kept[c][n] for c in chunks for n in (3, 0, 1, 2)]
    states = [prior[c][k][0] for c, k in jobs]
    old = [(n, mixed[c]) for n, c in enumerate(chunks) if c in mixed]

    def body(r, *refs):
        fields_in, refs = refs[: len(fields)], refs[len(fields) :]
        state_refs, refs = refs[: len(jobs)], refs[len(jobs) :]
        before, (*m_refs, square_ref, cross_ref) = refs[: len(sums)], refs[len(sums) :]
        square = before[0][...] if sums else jnp.zeros(square_ref.shape, F32)
        cross = before[1][...] if sums else jnp.zeros(cross_ref.shape, F32)
        for (c, piece), state in zip(jobs, state_refs, strict=True):
            n, offset = chunks.index(c), prior[c][piece][1]
            o_ref, q_ref, g_ref, gain_ref = fields_in[4 * n : 4 * n + 4]
            products = []
            for heads in pairs_of(layout.count):
                block = diagonal([state[rows_of(h, offset), :] for h in heads])
                both = dot(q_ref[piece, :, span(heads)], block, (1, 0))
                products += [both[:, lanes(m)] for m in range(len(heads))]
            for h in range(layout.count):
                at = (piece, slice(None), lanes(h))
                value = o_ref[at] + products[h]
                m_refs[n][at] = value
                square = square + value * value
                cross = cross + gain_ref[piece, :, lanes(h)] * g_ref[at].astype(F32) * value
        if final:
            inv = lax.rsqrt(jnp.sum(square, -1, keepdims=True) / layout.features + EPSILON)
            centered = jnp.sum(cross, -1, keepdims=True) / layout.features
            square = jnp.broadcast_to(inv, square.shape)
            cross = jnp.broadcast_to(inv * inv * inv * centered, cross.shape)
        square_ref[...] = square
        cross_ref[...] = cross

    *outs, square, cross = layout.call(
        "mix", body, rank, [], [*fields, *states, *sums],
        [(layout.kept(F32), None)] * len(chunks) + [(layout.narrow(), None)] * 2,
        into=[(a, n, pltpu.VMEM) for n, a in old], hint=hint,
    )
    return {**mixed, **dict(zip(chunks, outs, strict=True))}, [square, cross]


def mixed_gradients(layout, rank, mixed, queries, out_grad, gain, inv, factor):
    def body(r, m_ref, q_ref, g_ref, gain_ref, inv_ref, factor_ref, d_ref, *outs):
        piece = pl.program_id(0)

        def act(out):
            for h in range(layout.count):
                at = (piece, slice(None), lanes(h))
                scaled = gain_ref[piece, :, lanes(h)] * g_ref[at].astype(F32)
                grad = (inv_ref[...] * scaled - m_ref[at] * factor_ref[...]).astype(BF16)
                d_ref[at] = grad
                out[lanes(h), :] = dot(q_ref[at], grad, (0, 0)).astype(BF16)

        for_piece(outs, act)

    d_mixed, *states = layout.call(
        "mixed_gradients", body, rank, [], [mixed, queries, out_grad, gain, inv, factor],
        [(layout.kept(BF16), None)] + [(layout.piece(), None)] * layout.members,
        macs=layout.size * HD, moved=layout.size, grid=(layout.members,),
    )
    return d_mixed, states


def normed_output(layout, rank, mixed, out_grad, gain, inv, chunk, gain_grad, after):
    def body(r, m_ref, g_ref, gain_ref, inv_ref, o_ref, part_ref):
        for piece in range(layout.members):
            for h in range(layout.count):
                here = (piece, slice(None), lanes(h))
                normed = m_ref[here] * inv_ref[...]
                o_ref[here] = (normed * gain_ref[piece, :, lanes(h)]).astype(BF16)
                head = ((r[0] ^ piece) * layout.chunks + chunk) * layout.count + h
                part_ref[pl.ds(head, 1), :] = jnp.sum(g_ref[here].astype(F32) * normed, 0, keepdims=True)

    return layout.call(
        "normed_output", body, rank, [], [mixed, out_grad, gain, inv],
        [(layout.kept(BF16), None), (pltpu.VMEM((layout.heads, HD), F32), None)],
        into=[(a, 1, pltpu.VMEM) for a in gain_grad], after=after,
    )


def inner_gradients(
    layout, rank, weights, queries, keys, values, d_mixed, prior, chunk, part, own, after, ready=(), others=(), also=(), hint=0
):
    first, last = part
    targets = ([0] if ready else []) + ([1] if others else []) + ([2, 3] if also else [])
    hbm = [(layout.wide_shape(), HBM_WHOLE)] * len(targets)
    lists = [*((0, c, a) for c, a in ready), *((1, c, a) for c, a in others)]
    extra = max(len(also) - 4, 0)

    def body(r, *refs):
        w_refs, (q_ref, k_ref, v_ref, d_ref, *refs) = refs[: len(weights)], refs[len(weights) :]
        states, refs = refs[: last - first], refs[last - first :]
        list_refs, refs = refs[: len(lists)], refs[len(lists) :]
        also_refs, (dq_ref, dk_ref, dv_ref, token_ref, *refs) = refs[: len(also)], refs[len(also) :]
        hbm_refs, (state, dk_buffer, dv_buffer, sems) = dict(zip(targets, refs)), refs[len(hbm) :]
        step = pl.program_id(0)
        piece = step + first
        token_ref[...] = jnp.zeros_like(token_ref)

        def write(n, c, source, at):
            target = hbm_refs[n].at[:, layout.columns(r, at, c)]
            return pltpu.make_async_copy(source.at[at], target, sems.at[n * layout.chunks + c, at])

        def list_copies():
            for (n, c, _), ref in zip(lists, list_refs, strict=True):
                for at in range(layout.members):
                    yield write(n, c, ref, at)

        def outer_copies(at):
            return [write(n, 0, ref, at) for n, ref in ((2, dk_buffer), (3, dv_buffer))]

        @pl.when(step == 0)
        def _():
            for copy in list_copies():
                copy.start()

        for n, (ref, (_, offset)) in enumerate(zip(states, prior[first:last], strict=True)):

            @pl.when(step == n)
            def _(ref=ref, offset=offset):
                state[...] = ref[offset : offset + layout.count * HD, :]

        for n in range(extra):

            @pl.when(step == n)
            def _(n=n):
                store_outer(layout, also_refs[:4], also_refs[4 + n], 0, n, dk_buffer, dv_buffer, n)
                for copy in outer_copies(n):
                    copy.start()

        d_weights, from_prior = [], []
        for h in range(layout.count):
            at = (piece, slice(None), lanes(h))
            d_weights.append(masked_product(d_ref[at], v_ref[at], layout.cut()))
        for heads in pairs_of(layout.count):
            both = dot(d_ref[piece, :, span(heads)], diagonal([state[lanes(h), :] for h in heads]), (1, 1))
            from_prior += [both[:, lanes(n)] for n in range(len(heads))]
        for h in range(layout.count):
            at = (piece, slice(None), lanes(h))
            kept = [w_ref[piece, h] for w_ref in w_refs][: len(d_weights[h])]
            store_product(dq_ref, at, d_weights[h], k_ref[at], layout.cut(), from_prior[h])
            store_turned(dk_ref, at, d_weights[h], q_ref[at], layout.cut())
            store_turned(dv_ref, at, kept, d_ref[at], layout.cut())
        if others:

            @pl.when(step < last - first - 1)
            def _():
                write(1, chunk, dq_ref, piece).start()

        @pl.when(step == last - first - 1)
        def _():
            for copy in list_copies():
                copy.wait()
            for at in range(first, last - 1 if others else first):
                write(1, chunk, dq_ref, at).wait()
            for n in range(extra):
                for copy in outer_copies(n):
                    copy.wait()

    buffer = pltpu.VMEM((max(extra, 1), layout.tokens, layout.width), BF16)
    return layout.call(
        "inner_gradients", body, rank, [],
        [*weights, queries, keys, values, d_mixed, *[a for a, _ in prior[first:last]], *[a for _, _, a in lists], *also],
        [(layout.kept(BF16), None), (layout.kept(F32), None), (layout.kept(F32), None), (layout.token(), None)] + hbm,
        into=[(a, n, pltpu.VMEM) for n, a in enumerate(own)], after=after, hint=hint,
        scratch=[
            pltpu.VMEM((layout.count * HD, HD), BF16), buffer, buffer,
            pltpu.SemaphoreType.DMA((4 * layout.chunks, layout.members)),
        ],
        grid=(last - first,),
    )


def store_outer(layout, fields, state, offset, piece, dk_buffer, dv_buffer, slot):
    k_ref, v_ref, dki_ref, dvi_ref = fields
    sums = []
    for heads in pairs_of(layout.count):
        here = (piece, slice(None), span(heads))
        block = diagonal([state[rows_of(h, offset), :] for h in heads])
        sums.append((heads, here, dot(v_ref[here], block, (1, 1)), dot(k_ref[here], block, (1, 0))))
    for heads, here, dk, dv in sums:
        dk_buffer[slot, :, span(heads)] = (dki_ref[here] + dk).astype(BF16)
        dv_buffer[slot, :, span(heads)] = (dvi_ref[here] + dv).astype(BF16)


def pairwise(terms):
    while len(terms) > 1:
        terms = [a + b for a, b in zip(terms[::2], terms[1::2], strict=True)]
    return terms[0]


def outer_gradients(layout, rank, keys, values, own, later, jobs, into, extra, queries, query_grad):
    chunks = sorted({c for c, _ in jobs})
    fields = [a for c in chunks for a in (keys[c], values[c], *own[c][1:])]
    states = [later[c][k][0] for c, k in jobs]
    count, heads_all = len(jobs), layout.heads
    gain_out = [(jax.ShapeDtypeStruct((heads_all, HD), F32), HBM_WHOLE)] if extra else []

    def body(r, *refs):
        fields_in, refs = refs[: len(fields)], refs[len(fields) :]
        state_refs, (q_ref, dk_hbm, dv_hbm, dq_hbm, *refs) = refs[:count], refs[count:]
        gain_hbm, (dk_buffer, dv_buffer, gain_buffer, sems) = refs[: len(gain_out)], refs[len(gain_out) :]
        at = layout.columns(r, layout.members - 1, layout.chunks - 1)
        copies = [pltpu.make_async_copy(q_ref.at[layout.members - 1], dq_hbm.at[:, at], sems.at[3, 0])]
        copies[0].start()
        if extra:
            parts = []
            for _, n in sorted((piece, n) for n, (c, piece) in enumerate(jobs) if c == chunks[-1]):
                rows = state_refs[n][-2 * heads_all :, :].astype(F32)
                parts.append(rows[:heads_all] + rows[heads_all:])
            gain_buffer[...] = pairwise(parts)
            copies.append(pltpu.make_async_copy(gain_buffer, gain_hbm[0], sems.at[2, 0]))
            copies[-1].start()
        for n, ((c, piece), state) in enumerate(zip(jobs, state_refs, strict=True)):
            at, offset = layout.columns(r, piece, c), later[c][piece][1]
            here = 4 * chunks.index(c)
            store_outer(layout, fields_in[here : here + 4], state, offset, piece, dk_buffer, dv_buffer, n)
            copies.append(pltpu.make_async_copy(dk_buffer.at[n], dk_hbm.at[:, at], sems.at[0, n]))
            copies.append(pltpu.make_async_copy(dv_buffer.at[n], dv_hbm.at[:, at], sems.at[1, n]))
            copies[-2].start()
            copies[-1].start()
        for copy in copies:
            copy.wait()

    return layout.call(
        "outer_gradients", body, rank, [], [*fields, *states, queries],
        [(layout.wide_shape(), HBM_WHOLE)] * 3 + gain_out,
        into=[(a, n, pltpu.HBM) for n, a in enumerate(into)] + [(query_grad, 2, pltpu.HBM)],
        scratch=[pltpu.VMEM((count, layout.tokens, layout.width), BF16)] * 2
        + [pltpu.VMEM((heads_all, HD), F32), pltpu.SemaphoreType.DMA((4, count))],
    )


def swap(array, axis, size, k):
    return lax.ppermute(array, axis, [(c, c ^ k) for c in range(size)])


def gather_home(pieces, context):
    order = [*range(1, len(pieces))][-1:] + [*range(1, len(pieces) - 1)]
    got = {k: swap(pieces[k], "context", context, k) for k in order}
    return [pieces[0]] + [got[k] for k in range(1, len(pieces))]


def group_total(layout, rank, got, after):
    def body(r, *refs):
        *gots, total = refs
        total[...] = sum(g[...].astype(F32) for g in gots).astype(BF16)

    return layout.call(
        "group_total", body, rank, [], got, [(layout.piece(), None)], after=after, moved=layout.count * HD * HD * 10
    )[0]


def cross_groups(total, members, context, forward):
    bases = []
    for far in range(1, context // members):
        hop = far * members
        up = [(c, c + hop) for c in range(context - hop)]
        bases.append(lax.ppermute(total, "context", up if forward else [(b, a) for a, b in up]))
    return bases


def spread(layout, rank, got, bases, forward, after, joined=(), gain=(), hint=0):
    members, heads_all = layout.members, layout.heads
    extra = 2 * heads_all * len(gain)
    shift = layout.count * HD * len(joined)

    def body(r, *refs):
        gots, rest = refs[:members], refs[members:]
        lows, rest = rest[: len(bases)], rest[len(bases) :]
        joined_refs, rest = rest[: len(joined)], rest[len(joined) :]
        gains, outs = rest[: len(gain)], rest[len(gain) :]
        for n, ref in enumerate(joined_refs):
            outs[-1][n * layout.count * HD : (n + 1) * layout.count * HD, :] = ref[...]
        for h in range(layout.count):
            held = [g[rows_of(h), :].astype(F32) for g in gots]
            base = sum((low[rows_of(h), :].astype(F32) for low in lows), jnp.zeros((HD, HD), F32))
            for k in range(members):
                part = base
                for j in range(members):
                    if j != k:
                        one, other = r[0] ^ j, r[0] ^ k
                        ahead = one < other if forward else one > other
                        part = part + held[j] * ahead.astype(F32)
                outs[k][rows_of(h, shift if k == members - 1 else 0), :] = part.astype(BF16)
        for ref in gains:
            high = ref[...].astype(BF16)
            low = (ref[...] - high.astype(F32)).astype(BF16)
            for out in outs:
                rows = out.shape[0]
                out[rows - 2 * heads_all : rows - heads_all, :] = high
                out[rows - heads_all : rows, :] = low

    return layout.call(
        "spread", body, rank, [], [*got, *bases, *joined, *gain],
        [(layout.piece(extra), None)] * (members - 1) + [(layout.piece(extra + shift), None)], after=after,
        hint=hint,
    )


def scatter_back(layout, rank, got, bases, context, forward, mark, between, gain=None, hint=0):
    far, joined, pieces = layout.members - 1, [], []
    for c in range(layout.chunks):
        final = c == layout.chunks - 1
        mark = between(c, mark)
        rows = [gain()] if final and gain else []
        outs = spread(layout, rank, got[c], bases[c], forward, mark, joined if final else [], rows, hint)
        mark = [outs[0]]
        joined.append(outs[far])
        order = range(far if final else far - 1, 0, -1)
        moved = {k: swap(outs[k], "context", context, k) for k in order}
        pieces.append([(moved.get(k, outs[k]), 0) for k in range(layout.members)])
    if far:
        last = pieces[-1][far][0]
        for c, chunk in enumerate(pieces):
            chunk[far] = (last, c * layout.count * HD)
    return pieces, mark


def xor_steps(axis, size, stride):
    steps = []
    while stride < size:
        steps.append((axis, size, stride))
        stride *= 2
    return steps


def added(layout, rank, one, other, after):
    def body(r, one_ref, other_ref, out_ref):
        out_ref[...] = one_ref[...] + other_ref[...]

    return layout.call(
        "gain_sum", body, rank, [], [one, other], [(pltpu.VMEM(one.shape, F32), None)], after=after, moved=one.size * 12
    )[0]


def shards(dp, context, queries, keys, values, gain, out_grad):
    tokens, features = queries.shape[1:]
    members = divisor(context, (4, 2, 1))
    layout = Layout(tokens, features, members, CHUNKS)
    chunks = range(CHUNKS)
    place = (lax.axis_index("context") % members).astype(jnp.int32).reshape(1)
    q, k, v, g = (array[0] for array in (queries, keys, values, out_grad))
    gain_row = gain.reshape(1, features)

    k_kept, v_kept, got = [], [], []
    for c in chunks:
        k_c, v_c, states = block_states(layout, place, k, v, c)
        k_kept.append(k_c)
        v_kept.append(v_c)
        got.append(gather_home(states, context))
    inner, bases, mark = [], [], []
    for c in chunks:
        total = group_total(layout, place, got[c], mark)
        bases.append(cross_groups(total, members, context, True))
        inner.append(within_block(layout, place, q, g, gain_row, k_kept[c], v_kept[c], c, [total]))
        mark = [inner[c][3]]
    prior, mark = scatter_back(layout, place, got, bases, context, True, mark, lambda c, mark: mark)
    far = members - 1
    early = [(c, k) for c in chunks[:-1] for k in range(far)]
    middle = [(CHUNKS - 1, k) for k in range(far)] or [(c, 0) for c in chunks]
    late = [(c, far) for c in chunks] if far else []
    mixed, sums = {}, []
    for group, hint in zip((early, late, middle), MIX_HINTS, strict=True):
        if group:
            mixed, sums = mix(layout, place, inner, prior, group, mixed, sums, group == middle, hint)
    inv, factor = sums

    d_mixed, got = [], []
    for c in chunks:
        q_c, g_c, gain_c = inner[c][:3]
        d_c, states = mixed_gradients(layout, place, mixed[c], q_c, g_c, gain_c, inv, factor)
        d_mixed.append(d_c)
        got.append(gather_home(states, context))

    normed, own, gain_grad = {}, [[] for _ in chunks], []
    regular = dp & (dp - 1) == 0 and context & (context - 1) == 0
    steps = xor_steps("dp", dp, 1) + xor_steps("context", context, members) if regular else []

    def inner_job(mark, c, part, hint=0, **beside):
        result = inner_gradients(
            layout, place, inner[c][4:], inner[c][0], k_kept[c], v_kept[c], d_mixed[c], prior[c], c, part, own[c], mark,
            hint=hint, **beside,
        )
        *own[c], token = result[:4]
        return [token], result[4:]

    def gain_job(mark):
        nonlocal gain_grad
        if not steps:
            return mark
        axis, size, stride = steps.pop(0)
        gain_grad = [added(layout, place, *gain_grad, swap(*gain_grad, axis, size, stride), mark)]
        return gain_grad

    cuts = sorted({0, members // 4, members // 2, members})
    jobs = [(0, part) for part in zip(cuts[:-1], cuts[1:], strict=True)]
    bases, mark = [], [d_mixed[-1]]
    for c in chunks:
        _, g_c, gain_c = inner[c][:3]
        normed[c], *gain_grad = normed_output(layout, place, mixed[c], g_c, gain_c, inv, c, gain_grad, mark)
        mark = gain_grad
        if c == CHUNKS - 1:
            mark, _ = inner_job(mark, *jobs.pop(0))
            mark = gain_job(mark)
        total = group_total(layout, place, got[c], mark)
        mark = [total]
        bases.append(cross_groups(total, members, context, False))


    def between(c, mark):
        if jobs:
            job = jobs.pop(0)
            mark, _ = inner_job(mark, *job)
        mark = gain_job(mark)
        while c == CHUNKS - 1 and steps:
            mark = gain_job(mark)
        return mark

    gain = (lambda: gain_grad[0]) if regular else None
    later, mark = scatter_back(layout, place, got, bases, context, False, mark, between, gain, SPREAD_HINT)
    also = [k_kept[0], v_kept[0], *own[0][1:], *[later[0][k][0] for k in range(far)]]
    others = [(c, own[c][0]) for c in chunks[:-1]]
    mark, (output, query_grad, *outer) = inner_job(
        mark, CHUNKS - 1, (0, members), OUTER_HINT, ready=[*normed.items()], others=others, also=also if far else []
    )
    *outer, query_grad, total_gain = [
        *outer_gradients(layout, place, k_kept, v_kept, own, later, middle + late, outer, regular, own[-1][0], query_grad), None
    ][:4]
    if not regular:
        total_gain = lax.psum(gain_grad[0], ("dp", "context"))
    return output[None], query_grad[None], outer[0][None], outer[1][None], total_gain.reshape(features)


def solution(mesh):
    sharded = P("dp", "context", None)
    return jax.shard_map(
        functools.partial(shards, mesh.shape["dp"], mesh.shape["context"]),
        mesh=mesh,
        in_specs=(sharded, sharded, sharded, P(), sharded),
        out_specs=(sharded, sharded, sharded, sharded, P()),
        check_vma=False,
    )
```
